128 devices in a mesh: dp: 64 (over y, x, z_lo, core), tensor: 2 (over z_hi).
Axes of the slice: x: 4, y: 4, z: 4 (z_hi: 2, z_lo: 2; z = z_hi * 2 + z_lo), core: 2. Of those that a mesh axis runs over, the one named last changes fastest.
Arguments:
- layer_input: bfloat16 [16384, 2048], P(('dp', 'tensor')), may hold values from -6 to 6
- attn_scale: bfloat16 [2048], P('dp'), may hold values from 0.25 to 1.75
- query_weight: bfloat16 [2048, 2048], P('dp', 'tensor'), may hold values from -0.125 to 0.125
- key_weight: bfloat16 [2048, 2048], P('dp', 'tensor'), may hold values from -0.125 to 0.125
- value_weight: bfloat16 [2048, 2048], P('dp', 'tensor'), may hold values from -0.125 to 0.125
- output_weight: bfloat16 [2048, 2048], P('tensor', 'dp'), may hold values from -0.75 to 0.75
- mlp_scale: bfloat16 [2048], P('dp'), may hold values from 0.25 to 1.75
- gate_weight: bfloat16 [2048, 5504], P('dp', 'tensor'), may hold values from -0.125 to 0.125
- up_weight: bfloat16 [2048, 5504], P('dp', 'tensor'), may hold values from -0.125 to 0.125
- down_weight: bfloat16 [5504, 2048], P('tensor', 'dp'), may hold values from -0.078125 to 0.078125
- out_grad: bfloat16 [16384, 2048], P(('dp', 'tensor')), may hold values from -24 to 24
Outputs:
- layer_output: bfloat16 [16384, 2048], P(('dp', 'tensor'))
- input_grad: bfloat16 [16384, 2048], P(('dp', 'tensor'))
- attn_scale_grad: float32 [2048], P('dp')
- query_grad: float32 [2048, 2048], P('dp', 'tensor')
- key_grad: float32 [2048, 2048], P('dp', 'tensor')
- value_grad: float32 [2048, 2048], P('dp', 'tensor')
- output_grad: float32 [2048, 2048], P('tensor', 'dp')
- mlp_scale_grad: float32 [2048], P('dp')
- gate_grad: float32 [2048, 5504], P('dp', 'tensor')
- up_grad: float32 [2048, 5504], P('dp', 'tensor')
- down_grad: float32 [5504, 2048], P('tensor', 'dp')
The draws below stay inside these ranges and needn't reach their ends.
All inputs are finite; a program needn't handle non-finite values.
Results may differ from the reference program's by a relative error of at most 0.017.
Values may be sent and summed in bfloat16 or wider, within the bound.
No kernel may reach another device: no remote copies, remote signals or barrier semaphores. Data moves between devices by JAX's collectives and lax.ppermute only.
A program may use at most 256 MiB of HBM per device.

```python
import math
import jax
import jax.numpy as jnp
from jax import lax

D = 2048
HEADS = 16
HD = 128
FF = 5504
SEQ = 256
TOKENS = 16384
N_DP = 64


def raised(values, key, source, target, shards_of, factor):
    def block_of(dim):
        return (jnp.arange(values.shape[dim]) // (values.shape[dim] // shards_of)).reshape((-1,) + (1,) * (values.ndim - 1 - dim))

    one_side = jax.random.permutation(key, shards_of)[block_of(target)]
    far = (block_of(target) + shards_of // 2) % shards_of
    return jnp.where((block_of(source) == one_side) | (block_of(source) == far), factor * values, values)


def steps_of(stream_key, extent, cuts, smallest, top_value):
    def one(position, shards_of):
        steps = jax.random.uniform(jax.random.fold_in(jax.random.fold_in(stream_key, 6), position), (shards_of,), jnp.float32, smallest / len(cuts), top_value / len(cuts))
        return jnp.repeat(jnp.exp(steps), extent[position] // shards_of).reshape((-1,) + (1,) * (len(extent) - position - 1))

    loudness = one(*cuts[0])
    for cut in cuts[1:]:
        loudness = loudness * one(*cut)
    return loudness


def centred(own_key, shape, scale, bound, split=(), kind=jnp.bfloat16):
    factor_of = steps_of(own_key, shape, split, -0.22, 0.18) if split else 1.0
    entries = jax.random.normal(own_key, shape, jnp.float32) * scale * factor_of
    return jnp.minimum(jnp.maximum(entries, -bound), bound).astype(kind)


def bell_draw_with(stream_key, extent, deviation, bound, split, heavy, kind=jnp.bfloat16):
    values = deviation * jax.random.normal(stream_key, extent, jnp.float32)
    if split:
        values = values * steps_of(stream_key, extent, split, -0.22, 0.18)
    return jnp.clip(raised(values, jax.random.fold_in(stream_key, 3), *heavy), -bound, bound).astype(kind)


def setup_inputs(seed: int = 0) -> dict:
    arg_keys = jax.random.split(jax.random.key(seed), 12)
    return {
        "layer_input": centred(arg_keys[0], (TOKENS, D), 1.0, 6.0, ((0, 128),)),
        "attn_scale": jnp.clip(1.0 + 0.15 * jax.random.normal(arg_keys[1], (D,), jnp.float32), 0.25, 1.75).astype(jnp.bfloat16),
        "query_weight": centred(arg_keys[2], (D, D), D ** -0.5, 0.125, ((0, 64), (1, 2))),
        "key_weight": centred(arg_keys[3], (D, D), D ** -0.5, 0.125, ((0, 64), (1, 2))),
        "value_weight": centred(arg_keys[4], (D, D), D ** -0.5, 0.125, ((0, 64), (1, 2))),
        "output_weight": centred(arg_keys[5], (D, D), (D // 32) ** -0.5, 0.75, ((0, 2), (1, 64))),
        "mlp_scale": jnp.clip(1.0 + 0.15 * jax.random.normal(arg_keys[6], (D,), jnp.float32), 0.25, 1.75).astype(jnp.bfloat16),
        "gate_weight": centred(arg_keys[7], (D, FF), D ** -0.5, 0.125, ((0, 64), (1, 2))),
        "up_weight": centred(arg_keys[8], (D, FF), D ** -0.5, 0.125, ((0, 64), (1, 2))),
        "down_weight": centred(arg_keys[9], (FF, D), FF ** -0.5, 0.078125, ((0, 2), (1, 64))),
        "out_grad": bell_draw_with(arg_keys[10], (TOKENS, D), 1.0, 24.0, ((0, 128),), (0, 1, 128, 5.5)),
    }


@jax.custom_vjp
def low(v):
    return lax.optimization_barrier(v.astype(jnp.bfloat16)).astype(jnp.float32)

@jax.custom_vjp
def low_back(v):
    return v

def low_keep(v):
    return (low(v), None)

def low_pass(kept, grad):
    return (grad,)

def back_keep(v):
    return (v, None)

def back_low(kept, grad):
    return (low(grad),)
low.defvjp(low_keep, low_pass)
low_back.defvjp(back_keep, back_low)
epsilon = 1e-05
rope_base = 10000.0
masked_score = -1e+30
highest = lax.Precision.HIGHEST

def rms_norm(row_values, gain):
    inv_rms = lax.rsqrt(lax.optimization_barrier(jnp.mean(row_values * row_values, axis=-1, keepdims=True)) + epsilon)
    return row_values * inv_rms * gain

def rotary(values):
    length = values.shape[-3]
    half_size = values.shape[-1] // 2
    frequency = rope_base ** (-jnp.arange(half_size, dtype=jnp.float32) * 2.0 / values.shape[-1])
    angles = jnp.arange(length, dtype=jnp.float32)[:, None] * frequency[None, :]
    cosine_table = jnp.cos(angles)[:, None, :]
    sine_table = jnp.sin(angles)[:, None, :]
    first_half = values[..., :half_size]
    second_half = values[..., half_size:]
    return jnp.concatenate([first_half * cosine_table - second_half * sine_table, second_half * cosine_table + first_half * sine_table], axis=-1)

def attend(block):
    queries, key_rows, value_rows = block
    length = queries.shape[0]
    scores = low_back(jnp.einsum('qhd,khd->hqk', queries, key_rows, precision=highest) * (1.0 / math.sqrt(HD)))
    causal = jnp.arange(length)[:, None] >= jnp.arange(length)[None, :]
    scores = jnp.where(causal[None], scores, masked_score)
    row_max = lax.optimization_barrier(jnp.max(scores, axis=-1, keepdims=True))
    exp_scores = jnp.exp(scores - row_max)
    soft_weights = exp_scores / lax.optimization_barrier(jnp.sum(exp_scores, axis=-1, keepdims=True))
    return jnp.einsum('hqk,khd->qhd', low(soft_weights), value_rows, precision=highest)

def layer(layer_input, attn_scale, query_weight, key_weight, value_weight, output_weight, mlp_scale, gate_weight, up_weight, down_weight):
    normed_in = low(rms_norm(layer_input, attn_scale))

    def heads_of(weight):
        return jnp.dot(normed_in, weight, precision=highest).reshape(N_DP, SEQ, HEADS, HD)
    queries = low(rotary(low_back(heads_of(query_weight))))
    key_rows = low(rotary(low_back(heads_of(key_weight))))
    value_rows = low(low_back(heads_of(value_weight)))
    head_mix = lax.map(jax.checkpoint(attend), (queries, key_rows, value_rows))
    heads_cat = low(low_back(head_mix.reshape(N_DP * SEQ, HEADS * HD)))
    hidden_state = layer_input + low_back(jnp.dot(heads_cat, output_weight, precision=highest))
    normed_mid = low(rms_norm(hidden_state, mlp_scale))
    gate_pre = low_back(jnp.dot(normed_mid, gate_weight, precision=highest))
    up_pre = low_back(jnp.dot(normed_mid, up_weight, precision=highest))
    activation = low(gate_pre * jax.nn.sigmoid(gate_pre) * up_pre)
    return hidden_state + jnp.dot(activation, down_weight, precision=highest)

def reference(layer_input, attn_scale, query_weight, key_weight, value_weight, output_weight, mlp_scale, gate_weight, up_weight, down_weight, out_grad):
    inputs = [array.astype(jnp.float32) for array in (layer_input, attn_scale, query_weight, key_weight, value_weight, output_weight, mlp_scale, gate_weight, up_weight, down_weight)]
    layer_output, pullback = jax.vjp(layer, *inputs)
    grads = pullback(out_grad.astype(jnp.float32))
    return (layer_output.astype(jnp.bfloat16), grads[0].astype(jnp.bfloat16), grads[1], grads[2], grads[3], grads[4], grads[5], grads[6], grads[7], grads[8], grads[9])
```

```python
import math

import jax
import jax.numpy as jnp
from jax import lax
from jax.sharding import Mesh, PartitionSpec as P

HD = 128
EPSILON = 1e-05
ROPE_BASE = 10000.0
MASKED = -1e30
BF = jnp.bfloat16
F32 = jnp.float32

GROUP = ("y", "x", "l", "c")
RING = ("l", "t")
PLACES = (0, 2, 1, 3)


def plain(left, right):
    return jnp.dot(left, right, preferred_element_type=F32)


def times_t(left, right):
    return lax.dot_general(left, right, (((1,), (1,)), ((), ())), preferred_element_type=F32)


def left_t(left, right):
    return lax.dot_general(left, right, (((0,), (0,)), ((), ())), preferred_element_type=F32)


def move(values, axis, distance):
    place = PLACES if axis == RING else range(4)
    return lax.ppermute(values, axis, [(place[s], place[(s + distance) % 4]) for s in range(4)])


def swap(values, axis):
    return lax.ppermute(values, axis, [(0, 1), (1, 0)])


def gather_rows(own):
    back1 = move(own, RING, -1)
    back3 = move(own, RING, 1)
    back2 = move(own, RING, 2)
    mine = [own, back2, back1, back3]
    return jnp.concatenate(mine + [swap(block, "c") for block in mine], axis=0)


def scatter_rows(partial):
    rows = partial.shape[0] // 8
    other = swap(partial[4 * rows :], "c")
    blocks = partial[: 4 * rows].astype(F32) + other.astype(F32)
    to2, to1, to3 = (blocks[rows * i : rows * (i + 1)].astype(BF) for i in (1, 2, 3))
    got1 = move(to1, RING, 1)
    got3 = move(to3, RING, -1)
    got2 = move(to2, RING, 2)
    return blocks[:rows] + got1.astype(F32) + got3.astype(F32) + got2.astype(F32)


def exchange(pieces):
    core, low = lax.axis_index("c"), lax.axis_index("l")
    mine = jnp.where(core == 0, pieces[:, 0], pieces[:, 1])
    theirs = swap(jnp.where(core == 0, pieces[:, 1], pieces[:, 0]), "c")
    cores = jnp.stack(
        [jnp.where(core == 0, mine, theirs), jnp.where(core == 0, theirs, mine)], axis=1
    )
    mine = jnp.where(low == 0, cores[0], cores[1])
    theirs = swap(jnp.where(low == 0, cores[1], cores[0]), "l")
    return jnp.stack([jnp.where(low == 0, mine, theirs), jnp.where(low == 0, theirs, mine)], axis=0)


def split_pieces(weight, width):
    rows, columns = weight.shape
    pieces = weight.reshape(rows, 4, columns // 4)
    return jnp.pad(pieces, ((0, 0), (0, 0), (0, width - columns // 4)))


def to_pieces(weights, widths):
    joined = jnp.concatenate([split_pieces(w, n) for w, n in zip(weights, widths)], axis=2)
    rows = joined.shape[0]
    return joined.transpose(1, 0, 2).reshape(2, 2, rows, joined.shape[2])


def gather_line(block, axis):
    index = lax.axis_index(axis)
    found = jnp.zeros((4,) + block.shape, block.dtype)
    for distance, values in (
        (0, block),
        (1, move(block, axis, -1)),
        (3, move(block, axis, 1)),
        (2, move(block, axis, 2)),
    ):
        found = lax.dynamic_update_index_in_dim(found, values, (index + distance) % 4, 0)
    return found


def gather_plane(block, first):
    second = "x" if first == "y" else "y"
    index = lax.axis_index(second)
    line = gather_line(block, first)
    place = 0 if second == "y" else 1
    found = jnp.zeros((4, 4) + block.shape, block.dtype)
    for distance, values in (
        (0, line),
        (1, move(line, second, -1)),
        (3, move(line, second, 1)),
        (2, move(line, second, 2)),
    ):
        found = lax.dynamic_update_index_in_dim(found, values, (index + distance) % 4, place)
    return found.reshape(16 * block.shape[0], block.shape[1])


def reduce_line(blocks, axis, place):
    index = lax.axis_index(axis)

    def part(distance):
        return lax.dynamic_index_in_dim(blocks, (index + distance) % 4, place, keepdims=False)

    total = part(0).astype(F32)
    for distance in (1, 3, 2):
        total = total + move(part(distance), axis, distance).astype(F32)
    return total


def reduce_plane(partial, first):
    rows, columns = partial.shape
    blocks = partial.reshape(4, 4, rows // 16, columns)
    second = "x" if first == "y" else "y"
    line = reduce_line(blocks, first, 0 if first == "y" else 1).astype(BF)
    return reduce_line(line, second, 0)


def rms_unit(rows):
    inv = lax.rsqrt(jnp.mean(rows * rows, axis=-1, keepdims=True) + EPSILON)
    return rows * inv, inv


def rms_back(grad_unit, unit, inv):
    return inv * (grad_unit - unit * jnp.mean(grad_unit * unit, axis=-1, keepdims=True))


def positions(half):
    ring = lax.axis_index("t") * 2 + lax.axis_index("l")
    rows = jnp.arange(2 * half, dtype=jnp.int32)
    starts = jnp.stack([ring // 2, ((ring + 1) % 4) // 2]) * half
    return (rows[None, :] + starts[:, None]) % (2 * half)


def rotary_tables(place):
    half_size = HD // 2
    frequency = ROPE_BASE ** (-jnp.arange(half_size, dtype=F32) * 2.0 / HD)
    length = place.shape[-1]
    angles = jnp.arange(length, dtype=F32)[:, None] * frequency[None, :]
    tables = []
    for table in (jnp.cos(angles), jnp.sin(angles)):
        turned = jnp.roll(table, length // 2, axis=0)
        both = jnp.stack([jnp.where(place[i, 0] == 0, table, turned) for i in range(2)])
        tables.append(jnp.concatenate([both, both], axis=0))
    return tables


def rotate(values, cosine, sine):
    half_size = HD // 2
    first, second = values[..., :half_size], values[..., half_size:]
    return jnp.concatenate([first * cosine - second * sine, second * cosine + first * sine], -1)


def batched(left, right, left_dim, right_dim):
    return lax.dot_general(
        left, right, (((left_dim,), (right_dim,)), ((0,), (0,))), preferred_element_type=F32
    )


def shards(
    layer_input,
    attn_scale,
    query_weight,
    key_weight,
    value_weight,
    output_weight,
    mlp_scale,
    gate_weight,
    up_weight,
    down_weight,
    out_grad,
):
    half, width = layer_input.shape
    length = 2 * half
    tokens = 8 * half
    gain_attn = attn_scale.astype(F32)[:, None]
    gain_mlp = mlp_scale.astype(F32)[:, None]
    part = query_weight.shape[1] // 4
    heads = part // HD
    units = gate_weight.shape[1] // 4
    wide = -(-units // 128) * 128
    factor = 1.0 / math.sqrt(HD)

    def scaled(weight, gain):
        return (weight.astype(F32) * gain).astype(BF)

    attn_pieces = to_pieces(
        [
            scaled(query_weight, gain_attn),
            scaled(key_weight, gain_attn),
            scaled(value_weight, gain_attn),
            output_weight.T,
        ],
        [part] * 4,
    )
    mlp_pieces = to_pieces(
        [scaled(gate_weight, gain_mlp), scaled(up_weight, gain_mlp), down_weight.T], [wide] * 3
    )
    attn_block = exchange(attn_pieces).reshape(-1, 4 * part)
    qk_weight = gather_plane(attn_block[:, : 2 * part], "x")
    vo_weight = gather_plane(attn_block[:, 2 * part :], "y")
    mlp_block = exchange(mlp_pieces).reshape(-1, 3 * wide)
    mlp_weight = lax.all_gather(mlp_block, ("y", "x"), axis=0, tiled=True)
    gu_weight, down_t = mlp_weight[:, : 2 * wide], mlp_weight[:, 2 * wide :]

    unit_in, inv_in = rms_unit(layer_input.astype(F32))
    rows_in = gather_rows(unit_in.astype(BF))
    place = positions(half)
    cosine, sine = rotary_tables(place)
    causal = place[:, :, None] >= place[:, None, :]
    causal = jnp.concatenate([causal, causal], axis=0)
    qk = plain(rows_in, qk_weight)
    value_all = plain(rows_in, vo_weight[:, :part]).astype(BF).reshape(4, length, part)
    output_t = vo_weight[:, part:]

    def head(values, index):
        return values[:, index * HD : (index + 1) * HD].reshape(4, length, HD)

    kept, mixes = [], []
    for i in range(heads):
        query = rotate(head(qk[:, :part], i), cosine, sine).astype(BF)
        key = rotate(head(qk[:, part:], i), cosine, sine).astype(BF)
        value = value_all[:, :, i * HD : (i + 1) * HD]
        scores = jnp.where(causal, batched(query, key, 2, 2) * factor, MASKED)
        weights = jnp.exp(scores - jnp.max(scores, axis=-1, keepdims=True))
        soft = weights / jnp.sum(weights, axis=-1, keepdims=True)
        mixes.append(batched(soft.astype(BF), value, 2, 1).astype(BF))
        kept.append((query, key, value, soft))
    heads_cat = jnp.concatenate(mixes, axis=-1).reshape(tokens, part)
    hidden = layer_input.astype(F32) + scatter_rows(times_t(heads_cat, output_t).astype(BF))

    unit_mid, inv_mid = rms_unit(hidden)
    rows_mid = gather_rows(unit_mid.astype(BF))
    gate_up = plain(rows_mid, gu_weight)
    gate, up = gate_up[:, :wide], gate_up[:, wide:]
    sigmoid = jax.nn.sigmoid(gate)
    swish = gate * sigmoid
    activation = (swish * up).astype(BF)
    layer_output = (hidden + scatter_rows(times_t(activation, down_t).astype(BF))).astype(BF)

    rows_grad = gather_rows(out_grad)
    grad_act = plain(rows_grad, down_t)
    grad_gate = (grad_act * up * (sigmoid + swish * (1.0 - sigmoid))).astype(BF)
    grad_up = (grad_act * swish).astype(BF)
    grad_gu = jnp.concatenate([grad_gate, grad_up], axis=1)
    grad_unit_mid = scatter_rows(times_t(grad_gu, gu_weight).astype(BF))
    mlp_partial = jnp.concatenate([left_t(rows_mid, grad_gu), left_t(rows_grad, activation)], axis=1)
    mlp_sum = lax.psum_scatter(
        mlp_partial.astype(BF), ("y", "x"), scatter_dimension=0, tiled=True
    )
    grad_hidden = out_grad.astype(F32) + rms_back(grad_unit_mid, unit_mid, inv_mid)

    rows_hidden = gather_rows(grad_hidden.astype(BF))
    grad_heads = plain(rows_hidden, output_t).astype(BF)
    output_partial = left_t(rows_hidden, heads_cat)
    grad_q, grad_k, grad_v = [], [], []
    for i in range(heads):
        query, key, value, soft = kept[i]
        grad_mix = head(grad_heads, i)
        grad_soft = batched(grad_mix, value, 2, 2)
        grad_v.append(batched(soft.astype(BF), grad_mix, 1, 1).astype(BF))
        inner = jnp.sum(grad_soft * soft, axis=-1, keepdims=True)
        grad_scores = (soft * (grad_soft - inner)).astype(BF)
        back_q = batched(grad_scores, key, 2, 1) * factor
        back_k = batched(grad_scores, query, 1, 1) * factor
        grad_q.append(rotate(back_q, cosine, -sine).astype(BF))
        grad_k.append(rotate(back_k, cosine, -sine).astype(BF))
    grad_qk = jnp.concatenate(grad_q + grad_k, axis=-1).reshape(tokens, 2 * part)
    grad_value = jnp.concatenate(grad_v, axis=-1).reshape(tokens, part)
    qk_sum = reduce_plane(left_t(rows_in, grad_qk).astype(BF), "x")
    vo_partial = jnp.concatenate([left_t(rows_in, grad_value), output_partial], axis=1)
    vo_sum = reduce_plane(vo_partial.astype(BF), "y")
    grad_unit_in = scatter_rows(
        (times_t(grad_qk, qk_weight) + times_t(grad_value, vo_weight[:, :part])).astype(BF)
    )
    input_grad = (grad_hidden + rms_back(grad_unit_in, unit_in, inv_in)).astype(BF)

    def owned(total):
        return exchange(total.astype(BF).reshape(2, 2, -1, total.shape[1]))

    def whole(pieces, start, size):
        piece = pieces[..., start : start + size].reshape(4, -1, size)
        return piece.transpose(1, 0, 2).reshape(-1, 4 * size).astype(F32)

    mlp_own = owned(mlp_sum)
    attn_own = owned(jnp.concatenate([qk_sum, vo_sum], axis=1))
    gate_own, up_own, down_own = (whole(mlp_own, wide * i, units) for i in range(3))
    query_own, key_own, value_own, output_own = (whole(attn_own, part * i, part) for i in range(4))

    def gain_of(pairs):
        local = sum(jnp.sum(w.astype(F32) * g, axis=1) for w, g in pairs)
        return local + swap(local, "t")

    mlp_gain = gain_of([(gate_weight, gate_own), (up_weight, up_own)])
    attn_gain = gain_of(
        [(query_weight, query_own), (key_weight, key_own), (value_weight, value_own)]
    )
    return (
        layer_output,
        input_grad,
        attn_gain,
        query_own * gain_attn,
        key_own * gain_attn,
        value_own * gain_attn,
        output_own.T,
        mlp_gain,
        gate_own * gain_mlp,
        up_own * gain_mlp,
        down_own.T,
    )


def solution(mesh):
    devices = mesh.devices.reshape(4, 4, 2, 2, 2)
    fine = Mesh(devices, ("y", "x", "l", "c", "t"))
    rows = P(GROUP + ("t",), None)
    gain, into, out = P(GROUP), P(GROUP, "t"), P("t", GROUP)
    return jax.shard_map(
        shards,
        mesh=fine,
        in_specs=(rows, gain, into, into, into, out, gain, into, into, out, rows),
        out_specs=(rows, rows, gain, into, into, into, out, gain, into, into, out),
        check_vma=False,
    )
```

```python
import functools
import math

import jax
import jax.numpy as jnp
from jax import lax
from jax.experimental import pallas as pl
from jax.experimental.pallas import tpu as pltpu
from jax.sharding import Mesh, PartitionSpec as P

HD = 128
EPSILON = 1e-05
ROPE_BASE = 10000.0
MASKED = -1e30
BF = jnp.bfloat16
F32 = jnp.float32

GROUP = ("y", "x", "l", "c")
RING = ("l", "c", "t")


def plain(left, right):
    return jnp.dot(left, right, preferred_element_type=F32)


def times_t(left, right):
    return lax.dot_general(left, right, (((1,), (1,)), ((), ())), preferred_element_type=F32)


def left_t(left, right):
    return lax.dot_general(left, right, (((0,), (0,)), ((), ())), preferred_element_type=F32)


def swap(values, axis):
    return lax.ppermute(values, axis, [(0, 1), (1, 0)])


def hop(values):
    def place(z, core):
        return (z % 2) * 4 + core * 2 + z // 2

    pairs = []
    for z in range(4):
        pairs.append((place(z, 0), place((z + 1) % 4, 0)))
        pairs.append((place(z, 1), place((z + 3) % 4, 1)))
    return lax.ppermute(values, RING, pairs)


def after(values, *others):
    return lax.optimization_barrier((values, *others))[0]


EVEN = ((0, 0), (1, 0), (2, 0), (3, 0))
ODD = ((0, 0), (1, 1), (0, 1), (1, 0))


def gather_near(own):
    other = swap(own, "c")
    p = hop(jnp.concatenate([own, other], axis=0))
    return (own, other), (p, swap(p, "c"))


def gather_far(near, odd, *others):
    own, other = near
    far = hop(after(odd[0][: own.shape[0]], odd[1]))
    return (own, far, other, swap(after(far, *others), "c"))


def scatter_rows(even, odd, *others):
    rows = even[0].shape[0] // 2
    got = swap(even[1], "c")
    far = even[0][rows:].astype(F32) + got[rows:].astype(F32)
    relayed = hop(far.astype(BF))
    side = swap(odd[1], "c")
    mine = odd[0][:rows].astype(F32) + side[:rows].astype(F32) + relayed.astype(F32)
    other = odd[0][rows:].astype(F32) + side[rows:].astype(F32)
    last = hop(jnp.concatenate([mine.astype(BF), other.astype(BF)], axis=0))
    last = after(last, *others)
    crossed = swap(last[rows:], "c")
    total = even[0][:rows].astype(F32) + got[:rows].astype(F32)
    return total + last[:rows].astype(F32) + crossed.astype(F32)


def exchange(pieces):
    core, low = lax.axis_index("c"), lax.axis_index("l")
    mine = jnp.where(core == 0, pieces[:, 0], pieces[:, 1])
    theirs = swap(jnp.where(core == 0, pieces[:, 1], pieces[:, 0]), "c")
    cores = jnp.stack(
        [jnp.where(core == 0, mine, theirs), jnp.where(core == 0, theirs, mine)], axis=1
    )
    mine = jnp.where(low == 0, cores[0], cores[1])
    theirs = swap(jnp.where(low == 0, cores[1], cores[0]), "l")
    return jnp.stack([jnp.where(low == 0, mine, theirs), jnp.where(low == 0, theirs, mine)], axis=0)


def split_pieces(weight, width):
    rows, columns = weight.shape
    pieces = weight.reshape(rows, 4, columns // 4)
    return jnp.pad(pieces, ((0, 0), (0, 0), (0, width - columns // 4)))


def to_pieces(weights, widths):
    joined = jnp.concatenate([split_pieces(w, n) for w, n in zip(weights, widths)], axis=2)
    rows = joined.shape[0]
    return joined.transpose(1, 0, 2).reshape(2, 2, rows, joined.shape[2])


PLANE = ("y", "x", "c")


def along(values, distance, second):
    pairs = []
    for place in range(32):
        y, x, core = place // 8, place // 2 % 4, place % 2
        if (core == 0) != second:
            target = (y, (x + distance) % 4, core)
        else:
            target = ((y + distance) % 4, x, core)
        pairs.append((place, (target[0] * 4 + target[1]) * 2 + target[2]))
    return lax.ppermute(values, PLANE, pairs)


def gather_line(block):
    return jnp.stack([block] + [along(block, -d, False) for d in (1, 2, 3)])


def gather_plane(line):
    lines = [line] + [along(line, -d, True) for d in (1, 2, 3)]
    return lines + [swap(v, "c") for v in lines]


def reduce_plane(keep, send):
    got = swap(send, "c")
    parts = [jnp.concatenate([keep[d], got[d]], axis=-1) for d in range(4)]
    total = parts[0].astype(F32)
    for d in (1, 3, 2):
        total = total + along(parts[d], d, False).astype(F32)
    return total.astype(BF)


def reduce_line(line):
    total = line[0].astype(F32)
    for d in (1, 3, 2):
        total = total + along(line[d], d, True).astype(F32)
    return total


def rms_unit(rows):
    inv = lax.rsqrt(jnp.mean(rows * rows, axis=-1, keepdims=True) + EPSILON)
    return rows * inv, inv


def rms_back(grad_unit, unit, inv):
    return inv * (grad_unit - unit * jnp.mean(grad_unit * unit, axis=-1, keepdims=True))


def places(half):
    core = lax.axis_index("c")
    ring = lax.axis_index("t") * 2 + lax.axis_index("l")
    start = jnp.stack([ring // 2, ((ring + 3 - 2 * core) % 4) // 2]).astype(jnp.int32) * half
    length = 2 * half
    frequency = ROPE_BASE ** (-jnp.arange(HD // 2, dtype=F32) * 2.0 / HD)
    angles = jnp.arange(length, dtype=F32)[:, None] * frequency[None, :]
    cosine, sine = jnp.cos(angles), jnp.sin(angles)
    tables = []
    for i in range(2):
        for table in (jnp.concatenate([cosine] * 2, 1), jnp.concatenate([-sine, sine], 1)):
            tables.append(jnp.where(start[i] == 0, table, jnp.roll(table, half, axis=0)))
    spot = jnp.concatenate([start, jnp.stack([lax.axis_index(a) for a in ("c", "y", "x")])])
    return spot.astype(jnp.int32), tables[:2], tables[2:]


VMEM = pl.BlockSpec(memory_space=pltpu.VMEM)
HBM = pl.BlockSpec(memory_space=pltpu.HBM)
SMEM = pl.BlockSpec(memory_space=pltpu.SMEM)


LIMIT = pltpu.CompilerParams(vmem_limit_bytes=40 * 2**20)


def kernel_call(body, shapes, flops, args, specs, scratch, name):
    moved = sum(a.size for a in args) + sum(math.prod(shape) for shape in shapes)
    return pl.pallas_call(
        body,
        out_shape=[jax.ShapeDtypeStruct(shape, BF) for shape in shapes],
        in_specs=specs,
        out_specs=[VMEM] * len(shapes),
        scratch_shapes=list(scratch),
        compiler_params=LIMIT,
        cost_estimate=pl.CostEstimate(
            flops=flops, bytes_accessed=2 * moved if flops else 0, transcendentals=0
        ),
        name=name,
    )(*args)


def wait_all(copies):
    for copy in copies:
        copy.wait()


def causal_mask(start, length):
    def place(dim):
        index = lax.broadcasted_iota(jnp.int32, (length, length), dim) + start
        return jnp.where(index >= length, index - length, index)

    return place(0) >= place(1)


def soft_weights(query, key, mask):
    scores = jnp.where(mask, times_t(query, key) * (1.0 / math.sqrt(HD)), MASKED)
    weights = jnp.exp(scores - jnp.max(scores, axis=-1, keepdims=True))
    return weights / jnp.sum(weights, axis=-1, keepdims=True)


def turned(values, cosine, sine):
    return values * cosine + pltpu.roll(values, HD // 2, 1) * sine


def fetch(pairs, sems, first=0):
    copies = [pltpu.make_async_copy(a, b, sems.at[first + i]) for i, (a, b) in enumerate(pairs)]
    for copy in copies:
        copy.start()
    return copies


def joined(arrays, slots, target, first=0):
    rows = sum(array.shape[0] for array in arrays) // 4
    return [
        (arrays[i].at[pl.ds(rows * j, rows), :], target.at[pl.ds(first + rows * n, rows), :])
        for n, (i, j) in enumerate(slots)
    ]


def feature_block(core, y, x, first, second):
    dy, dx = jnp.where(core == 0, second, first), jnp.where(core == 0, first, second)
    return lax.rem(y + dy, 4) * 4 + lax.rem(x + dx, 4)


def plane_blocks(spot, lines, target):
    core, y, x = spot[2], spot[3], spot[4]
    rows, size = lines[0].shape[1], lines[0].shape[2] // 2
    half = pl.ds(pl.multiple_of(core * size, size), size)
    pairs = []
    for kind, group in ((core, lines[:4]), (1 - core, lines[4:])):
        columns = pl.ds(pl.multiple_of(kind * size, size), size)
        for second in range(4):
            for first in range(4):
                row = pl.multiple_of(feature_block(kind, y, x, first, second) * rows, rows)
                source = group[second].at[first, :, half]
                pairs.append((source, target.at[pl.ds(row, rows), columns]))
    return pairs


OUTS = {EVEN: ((0, 0), (0, 1), (1, 0), (1, 1)), ODD: ((1, 1), (0, 0), (1, 0), (0, 1))}


def product_t(left, weight, targets, slots, chunk):
    rows = left.shape[0] // 4

    def step(i, carry):
        part = pl.ds(pl.multiple_of(i * chunk, chunk), chunk)
        found = times_t(left[...], weight[part, :]).astype(BF)
        for n, (target, block) in enumerate(OUTS[slots]):
            place = slice(rows * block, rows * (block + 1))
            targets[target][place, part] = found[rows * n : rows * (n + 1)]
        return carry

    lax.fori_loop(0, weight.shape[0] // chunk, step, 0)


def attend_kernel(slots, spot, *refs):
    n = len(refs) - 17
    arrays, lines, (cosine, sine) = refs[:n], refs[n : n + 8], refs[n + 8 : n + 10]
    qkv, heads_cat, kept, sent, rows, weight, sems = refs[n + 10 :]
    part = weight.shape[1] // 4
    length = cosine.shape[0]
    copies = fetch(joined(arrays, slots, rows) + plane_blocks(spot, lines, weight), sems)
    wait_all(copies)
    both = plain(rows[...], weight[:, : 3 * part])
    qkv[:, 2 * part :] = both[:, 2 * part :].astype(BF)
    mask = causal_mask(spot[0 if slots is EVEN else 1], length)
    for s in range(2):
        here = slice(s * length, (s + 1) * length)
        for i in range(part // HD):
            columns = slice(i * HD, (i + 1) * HD)
            others = slice(part + i * HD, part + (i + 1) * HD)
            values = slice(2 * part + i * HD, 2 * part + (i + 1) * HD)
            query = turned(both[here, columns], cosine[...], sine[...]).astype(BF)
            key = turned(both[here, others], cosine[...], sine[...]).astype(BF)
            qkv[here, columns] = query
            qkv[here, others] = key
            soft = soft_weights(query, key, mask).astype(BF)
            heads_cat[here, columns] = plain(soft, qkv[here, values]).astype(BF)
    product_t(heads_cat, weight.at[:, 3 * part :], (kept, sent), slots, 512)


def size_of(arrays):
    return sum(array.shape[0] for array in arrays), arrays[0].shape[1]


def attend(slots, spot, arrays, lines, tables):
    rows, width = size_of(arrays)
    part = lines[0].shape[2] // 4
    return kernel_call(
        functools.partial(attend_kernel, slots),
        [(rows, 3 * part), (rows, part), (rows // 2, width), (rows // 2, width)],
        0 if slots is ODD else 2 * rows * width * 4 * part,
        (spot, *arrays, *lines, *tables),
        [SMEM] + [HBM] * (len(arrays) + 8) + [VMEM] * 2,
        [
            pltpu.VMEM((rows, width), BF),
            pltpu.VMEM((width, 4 * part), BF),
            pltpu.SemaphoreType.DMA((36,)),
        ],
        name="attend",
    )


def attend_back_kernel(slots, spot, *refs):
    n = len(refs) - 17
    arrays, lines, (qkv, cosine, sine) = refs[:n], refs[n : n + 8], refs[n + 8 : n + 11]
    grad_qkv, kept, sent, rows, weight, sems = refs[n + 11 :]
    part = weight.shape[1] // 4
    length = cosine.shape[0]
    factor = 1.0 / math.sqrt(HD)
    copies = fetch(joined(arrays, slots, rows) + plane_blocks(spot, lines, weight), sems)
    for copy in copies:
        copy.wait()
    grad_heads = plain(rows[...], weight[:, 3 * part :]).astype(BF)
    mask = causal_mask(spot[0 if slots is EVEN else 1], length)
    for s in range(2):
        here = slice(s * length, (s + 1) * length)
        for i in range(part // HD):
            columns = slice(i * HD, (i + 1) * HD)
            others = slice(part + i * HD, part + (i + 1) * HD)
            values = slice(2 * part + i * HD, 2 * part + (i + 1) * HD)
            query, key = qkv[here, columns], qkv[here, others]
            soft = soft_weights(query, key, mask)
            grad_mix = grad_heads[here, columns]
            grad_soft = times_t(grad_mix, qkv[here, values])
            grad_qkv[here, values] = left_t(soft.astype(BF), grad_mix).astype(BF)
            inner = jnp.sum(grad_soft * soft, axis=-1, keepdims=True)
            grad_scores = (soft * (grad_soft - inner)).astype(BF)
            back_q = plain(grad_scores, key) * factor
            back_k = left_t(grad_scores, query) * factor
            grad_qkv[here, columns] = turned(back_q, cosine[...], -sine[...]).astype(BF)
            grad_qkv[here, others] = turned(back_k, cosine[...], -sine[...]).astype(BF)
    product_t(grad_qkv, weight.at[:, : 3 * part], (kept, sent), slots, 512)


def attend_back(slots, spot, arrays, qkv, lines, tables):
    rows, width = size_of(arrays)
    part = lines[0].shape[2] // 4
    return kernel_call(
        functools.partial(attend_back_kernel, slots),
        [(rows, 3 * part), (rows // 2, width), (rows // 2, width)],
        0 if slots is ODD else 2 * rows * width * 4 * part,
        (spot, *arrays, *lines, qkv, *tables),
        [SMEM] + [HBM] * (len(arrays) + 8) + [VMEM] * 3,
        [
            pltpu.VMEM((rows, width), BF),
            pltpu.VMEM((width, 4 * part), BF),
            pltpu.SemaphoreType.DMA((36,)),
        ],
        name="attend_back",
    )


def feed_kernel(slots, *refs):
    n = (len(refs) - 10) // 2
    arrays, gradients, source = refs[:n], refs[n : 2 * n], refs[2 * n]
    activation, grad_gu, kept, sent, grad_kept, grad_sent, rows, grads, weight, sems = refs[2 * n + 1 :]
    wide = weight.shape[1] // 3
    chunk = min(256, wide)
    first_copies = fetch(joined(arrays, slots, rows), sems)
    chunks = wide // chunk
    weight_copies = []
    for i in range(chunks):
        parts = [pl.ds(wide * j + chunk * i, chunk) for j in range(3)]
        pairs = [(source.at[:, part], weight.at[:, part]) for part in parts]
        weight_copies.append(fetch(pairs, sems, 8 + 3 * i))
        if i == 0:
            weight_copies[0] += fetch(joined(gradients, slots, grads), sems, 4)
    for copy in first_copies:
        copy.wait()
    for i in range(chunks):
        for copy in weight_copies[i]:
            copy.wait()
        first, second, third = (
            slice(wide * j + chunk * i, wide * j + chunk * (i + 1)) for j in range(3)
        )
        gate = plain(rows[...], weight[:, first])
        up = plain(rows[...], weight[:, second])
        grad_act = plain(grads[...], weight[:, third])
        sigmoid = jax.nn.sigmoid(gate)
        swish = gate * sigmoid
        activation[:, first] = (swish * up).astype(BF)
        grad_gu[:, first] = (grad_act * up * (sigmoid + swish * (1.0 - sigmoid))).astype(BF)
        grad_gu[:, second] = (grad_act * swish).astype(BF)
    product_t(activation, weight.at[:, 2 * wide :], (kept, sent), slots, 512)
    product_t(grad_gu, weight.at[:, : 2 * wide], (grad_kept, grad_sent), slots, 512)


def feed(slots, arrays, grads, weight):
    rows, width = size_of(arrays)
    wide = weight.shape[1] // 3
    return kernel_call(
        functools.partial(feed_kernel, slots),
        [(rows, wide), (rows, 2 * wide)] + [(rows // 2, width)] * 4,
        0 if slots is ODD else 2 * rows * width * 6 * wide,
        (*arrays, *grads, weight),
        [HBM] * (2 * len(arrays) + 1),
        [pltpu.VMEM((rows, width), BF)] * 2
        + [pltpu.VMEM((width, 3 * wide), BF), pltpu.SemaphoreType.DMA((17,))],
        name="feed",
    )


def feed_weights_kernel(*refs):
    grad_gus, activations, out = refs[12:14], refs[14:16], refs[16]
    rows, grads, grad_gu, activation, staged, sems = refs[17:]
    pairs = []
    for arrays, target in ((refs[:6], rows), (refs[6:12], grads)):
        middle = target.shape[0] // 2
        pairs += joined(arrays[:4], EVEN, target) + joined(arrays[4:], ODD, target, middle)
    for halves, target in ((grad_gus, grad_gu), (activations, activation)):
        middle = target.shape[0] // 2
        pairs += [(half, target.at[pl.ds(middle * i, middle), :]) for i, half in enumerate(halves)]
    copies = fetch(pairs, sems)
    wait_all(copies[:8] + copies[16:18])
    tile, split = 256, grad_gu.shape[1]
    tiles = rows.shape[1] // tile
    outs = []
    for i in range(tiles):
        part = slice(tile * i, tile * (i + 1))
        staged[part, :split] = left_t(rows[:, part], grad_gu[...]).astype(BF)
        if i == 0:
            wait_all(copies[8:16] + copies[18:])
        staged[part, split:] = left_t(grads[:, part], activation[...]).astype(BF)
        place = pl.ds(tile * i, tile)
        outs += fetch([(staged.at[place, :], out.at[place, :])], sems, 20 + i)
    wait_all(outs)


def feed_weights(even, odd, grads_even, grads_odd, first_right, second_right):
    rows, width = even[0].shape
    columns = [first_right[0].shape[1], second_right[0].shape[1]]
    args = (*even, *odd, *grads_even, *grads_odd, *first_right, *second_right)
    shapes = [(8 * rows, width)] * 2 + [(8 * rows, n) for n in columns] + [(width, sum(columns))]
    return pl.pallas_call(
        feed_weights_kernel,
        out_shape=jax.ShapeDtypeStruct((width, sum(columns)), BF),
        in_specs=[HBM] * 16,
        out_specs=HBM,
        scratch_shapes=[pltpu.VMEM(shape, BF) for shape in shapes]
        + [pltpu.SemaphoreType.DMA((20 + width // 256,))],
        compiler_params=LIMIT,
        cost_estimate=pl.CostEstimate(
            flops=16 * rows * width * sum(columns),
            bytes_accessed=2 * (16 * rows * width + width * sum(columns)),
            transcendentals=0,
        ),
        name="feed_weights",
    )(*args)


def attend_weights_kernel(spot, *refs):
    grads, heads, keep, send, ins, hiddens, sems = refs[12:14], refs[14:16], *refs[16:]
    pairs = []
    for arrays, target in ((refs[:6], ins), (refs[6:12], hiddens)):
        middle = target.shape[0] // 2
        pairs += joined(arrays[:4], EVEN, target) + joined(arrays[4:], ODD, target, middle)
    for copy in fetch(pairs, sems):
        copy.wait()
    tile, size = keep.shape[2:]

    def step(n, carry):
        i, j = lax.div(n, 2), lax.rem(n, 2) * 2
        columns = []
        for second in (j, j + 1):
            block = feature_block(spot[2], spot[3], spot[4], i, second)
            columns.append(pl.ds(pl.multiple_of(block * tile, tile), tile))
        found = []
        for rows, rights in ((ins, grads), (hiddens, heads)):
            left = jnp.concatenate([rows[:, c] for c in columns], axis=1)
            right = jnp.concatenate([r[...] for r in rights], axis=0)
            found.append(left_t(left, right).astype(BF))
        both = jnp.concatenate(found, axis=1)
        first, second = both[:, :size], both[:, size:]
        kept = jnp.where(spot[2] == 0, first, second)
        sent = jnp.where(spot[2] == 0, second, first)
        for k in range(2):
            keep[i, j + k] = kept[tile * k : tile * (k + 1)]
            send[j + k, i] = sent[tile * k : tile * (k + 1)]
        return carry

    lax.fori_loop(0, 8, step, 0)


def attend_weights(spot, ins, hiddens, grads, heads):
    rows, width = ins[0].shape
    tile = width // 16
    size = (grads[0].shape[1] + heads[0].shape[1]) // 2
    return kernel_call(
        attend_weights_kernel,
        [(4, 4, tile, size)] * 2,
        32 * rows * width * size,
        (spot, *ins, *hiddens, *grads, *heads),
        [SMEM] + [HBM] * 12 + [VMEM] * 4,
        [pltpu.VMEM((8 * rows, width), BF)] * 2 + [pltpu.SemaphoreType.DMA((16,))],
        name="attend_weights",
    )


def shards(
    layer_input,
    attn_scale,
    query_weight,
    key_weight,
    value_weight,
    output_weight,
    mlp_scale,
    gate_weight,
    up_weight,
    down_weight,
    out_grad,
):
    half, width = layer_input.shape
    gain_attn = attn_scale.astype(F32)[:, None]
    gain_mlp = mlp_scale.astype(F32)[:, None]
    part = query_weight.shape[1] // 4
    units = gate_weight.shape[1] // 4
    wide = -(-units // 128) * 128

    def scaled(weight, gain):
        return (weight.astype(F32) * gain).astype(BF)

    low_rows = query_weight.shape[0]
    attn_columns = [
        w.reshape(low_rows, 2, 2, part)
        for w in (
            scaled(query_weight, gain_attn),
            scaled(key_weight, gain_attn),
            scaled(value_weight, gain_attn),
            output_weight.T,
        )
    ]
    attn_pieces = jnp.stack(
        [jnp.concatenate(attn_columns[i : i + 2], axis=3) for i in (0, 2)], axis=1
    )
    attn_pieces = attn_pieces.reshape(low_rows, 2, 2, 4 * part).transpose(2, 1, 0, 3)
    mlp_pieces = to_pieces(
        [scaled(gate_weight, gain_mlp), scaled(up_weight, gain_mlp), down_weight.T], [wide] * 3
    )
    own_in = layer_input.astype(F32)
    unit_in, inv_in = rms_unit(own_in)
    near_in, odd_in = gather_near(unit_in.astype(BF))
    attn_block = exchange(attn_pieces).reshape(-1, 4 * part)
    attn_line = gather_line(attn_block)
    mlp_block = exchange(after(mlp_pieces, attn_block)).reshape(-1, 3 * wide)
    lines = gather_plane(attn_line)
    mlp_weight = lax.all_gather(
        after(mlp_block, lines[1], odd_in[0]), ("y", "x"), axis=0, tiled=True
    )
    near_grad, odd_grad = gather_near(after(out_grad, odd_in[0]))

    spot, even_tables, odd_tables = places(half)
    odd_at = attend(ODD, spot, after(odd_in, odd_grad[0]), lines, odd_tables)
    even_in = gather_far(near_in, odd_in)
    even_grad = gather_far(near_grad, odd_grad)
    even_at = attend(EVEN, spot, after(even_in, even_grad[1]), lines, even_tables)
    hidden = own_in + scatter_rows(even_at[2:], odd_at[2:])

    unit_mid, inv_mid = rms_unit(hidden)
    near_mid, odd_mid = gather_near(unit_mid.astype(BF))
    odd_feed = feed(ODD, odd_mid, odd_grad, mlp_weight)
    even_mid = gather_far(near_mid, odd_mid, odd_feed[0])
    even_feed = feed(EVEN, even_mid, even_grad, mlp_weight)
    mlp_partial = feed_weights(
        even_mid,
        odd_mid,
        even_grad,
        odd_grad,
        (even_feed[1], odd_feed[1]),
        (even_feed[0], odd_feed[0]),
    )
    grad_unit_mid = scatter_rows(even_feed[4:], odd_feed[4:], mlp_partial)
    grad_hidden = out_grad.astype(F32) + rms_back(grad_unit_mid, unit_mid, inv_mid)

    near_hidden, odd_hidden = gather_near(grad_hidden.astype(BF))
    mlp_sum = lax.psum_scatter(
        after(mlp_partial, near_hidden[1]), ("y", "x"), scatter_dimension=0, tiled=True
    )
    odd_back = attend_back(ODD, spot, odd_hidden, odd_at[0], lines, odd_tables)
    even_hidden = gather_far(near_hidden, odd_hidden, odd_back[0])
    even_back = attend_back(EVEN, spot, even_hidden, even_at[0], lines, even_tables)
    out_even, out_odd = after((even_feed[2:4], odd_feed[2:4]), even_hidden[1])
    keep, send = attend_weights(
        spot,
        even_in + odd_in,
        even_hidden + odd_hidden,
        (even_back[0], odd_back[0]),
        (even_at[1], odd_at[1]),
    )
    layer_output = (hidden + scatter_rows(out_even, out_odd, keep)).astype(BF)
    back_kept, back_sent = after((even_back[1], even_back[2]), layer_output)
    grad_unit_in = scatter_rows((back_kept, back_sent), odd_back[1:])
    input_grad = (grad_hidden + rms_back(grad_unit_in, unit_in, inv_in)).astype(BF)

    def whole(pieces, start, size):
        piece = pieces[..., start : start + size].reshape(4, -1, size)
        return piece.transpose(1, 0, 2).reshape(-1, 4 * size).astype(F32)

    def gain_of(pairs):
        local = sum(jnp.sum(w.astype(F32) * g, axis=1) for w, g in pairs)
        return local + swap(local, "t")

    mlp_own = exchange(mlp_sum.reshape(2, 2, -1, 3 * wide))
    gate_own, up_own, down_own = (whole(mlp_own, wide * i, units) for i in range(3))
    mlp_gain = gain_of([(gate_weight, gate_own), (up_weight, up_own)])
    attn_line = reduce_plane(keep, send)
    attn_line, input_grad, layer_output, gate_own, up_own, down_own, mlp_gain = (
        lax.optimization_barrier(
            (
                attn_line,
                input_grad,
                layer_output,
                gate_own * gain_mlp,
                up_own * gain_mlp,
                down_own,
                mlp_gain,
            )
        )
    )
    size = 2 * part
    core = lax.axis_index("c")
    attn_sum = reduce_line(attn_line)
    attn_sum = jnp.where(core == 0, attn_sum, jnp.roll(attn_sum, size, axis=1)).astype(BF)
    attn_own = exchange(attn_sum.reshape(2, 2, -1, 2 * size))

    def attn_whole(kind, start):
        piece = attn_own[:, kind].reshape(2, low_rows, 2, size)[..., start : start + part]
        return piece.transpose(1, 0, 2, 3).reshape(low_rows, 4 * part).astype(F32)

    query_own, key_own, value_own, output_own = (
        attn_whole(kind, start) for kind in (0, 1) for start in (0, part)
    )
    attn_gain = gain_of(
        [(query_weight, query_own), (key_weight, key_own), (value_weight, value_own)]
    )
    return (
        layer_output,
        input_grad,
        attn_gain,
        query_own * gain_attn,
        key_own * gain_attn,
        value_own * gain_attn,
        output_own.T,
        mlp_gain,
        gate_own,
        up_own,
        down_own.T,
    )


def solution(mesh):
    devices = mesh.devices.reshape(4, 4, 2, 2, 2)
    fine = Mesh(devices, ("y", "x", "l", "c", "t"))
    rows = P(GROUP + ("t",), None)
    gain, into, out = P(GROUP), P(GROUP, "t"), P("t", GROUP)
    return jax.shard_map(
        shards,
        mesh=fine,
        in_specs=(rows, gain, into, into, into, out, gain, into, into, out, rows),
        out_specs=(rows, rows, gain, into, into, into, out, gain, into, into, out),
        check_vma=False,
    )
```

```python
import functools
import math

import jax
import jax.numpy as jnp
from jax import lax
from jax.experimental import pallas as pl
from jax.experimental.pallas import tpu as pltpu
from jax.sharding import Mesh, PartitionSpec as P

HD = 128
EPSILON = 1e-05
ROPE_BASE = 10000.0
MASKED = -1e30
BF = jnp.bfloat16
F32 = jnp.float32

GROUP = ("y", "x", "l", "c")
RING = ("l", "c", "t")


def plain(left, right):
    return jnp.dot(left, right, preferred_element_type=F32)


def times_t(left, right):
    return lax.dot_general(left, right, (((1,), (1,)), ((), ())), preferred_element_type=F32)


def left_t(left, right):
    return lax.dot_general(left, right, (((0,), (0,)), ((), ())), preferred_element_type=F32)


def swap(values, axis):
    return lax.ppermute(values, axis, [(0, 1), (1, 0)])


def hop(values):
    def place(z, core):
        return (z % 2) * 4 + core * 2 + z // 2

    pairs = []
    for z in range(4):
        pairs.append((place(z, 0), place((z + 1) % 4, 0)))
        pairs.append((place(z, 1), place((z + 3) % 4, 1)))
    return lax.ppermute(values, RING, pairs)


def after(values, *others):
    return lax.optimization_barrier((values, *others))[0]


def stage(*values):
    return lax.optimization_barrier(values)


OPT = dict(
    g_after="far", g_before="rs1", ka_odd=0, ka_even=2, fd_odd=0, fd_even=8, kd_odd=0, kd_even=0, ke=0,
    kca_us=3, kcb_us=1, kca_at="r1", rs1_early=0, rs2_early=0, m_pair=0, h_pair=0, g_pair=1, nb60=1,
    feed_far=1, kd_far=1, far_s=1, t2mlp=0, pack=0, fold=1, t2p=1, low=1,  t4s=0, u2out=0, u3out=0, down_first=1, rs_tie="last", u1out=0, u3in=1, u3mlp=1, u4mlp=1, in_cat=1, out_cat=1, ka_far=0,
)
EVEN, ODD = "even", "odd"


def gather_odd(rows, pair=False, *others):
    other = swap(rows, "c")
    half = rows.shape[0]
    if pair:
        p = hop(after(jnp.concatenate([rows, other]), *others))
        s = swap(p, "c")
        p_mine, p_other, s_other, s_mine = p[:half], p[half:], s[:half], s[half:]
    else:
        p_mine, p_other = hop(after(rows, *others)), hop(after(other, *others))
        s_mine, s_other = swap(p_other, "c"), swap(p_mine, "c")
    return (rows, other), (p_mine, s_mine, p_other, s_other)


def gather_far(near, odd, *others):
    own, other = near
    far = hop(after(odd[0], odd[1], odd[3]) if OPT["far_s"] else odd[0])
    return (own, far, other, swap(after(far, *others), "c"))


def far_sum(even, got):
    rows = got.shape[0] // 2
    return (even[0][rows:].astype(F32) + got[rows:].astype(F32)).astype(BF)


def near_sums(odd, side, relayed):
    rows = relayed.shape[0]
    mine = odd[0][:rows].astype(F32) + side[:rows].astype(F32) + relayed.astype(F32)
    other = odd[0][rows:].astype(F32) + side[rows:].astype(F32)
    return mine.astype(BF), other.astype(BF)


def group_sum(even, odd, early, between=(), *others):
    rows = even[0].shape[0] // 2
    side = swap(odd[1], "c")
    other = hop((odd[0][rows:].astype(F32) + side[rows:].astype(F32)).astype(BF))
    got = swap(after(even[1], other) if early == 2 else even[1], "c")
    far = far_sum(even, got)
    if OPT["fold"]:
        own = even[0][:rows].astype(F32) + got[:rows].astype(F32)
        far, own = stage(far, own)
    relayed = hop(after(far, other) if early == 1 else far)
    relayed = after(relayed, *between) if between else relayed
    mine = odd[0][:rows].astype(F32) + side[:rows].astype(F32) + relayed.astype(F32)
    mine, other = after([hop(mine.astype(BF)), other], *others)
    crossed = swap(other, "c")
    return (own, mine, crossed) if OPT["fold"] else (even[0], got, mine, crossed)


def total(terms):
    rows = terms[-2].shape[0]
    return sum(term[:rows].astype(F32) for term in terms)


VMEM = pl.BlockSpec(memory_space=pltpu.VMEM)
SMEM = pl.BlockSpec(memory_space=pltpu.SMEM)


def small_call(body, shapes, args, name):
    return pl.pallas_call(
        body,
        out_shape=shapes,
        in_specs=[SMEM] + [VMEM] * (len(args) - 1),
        out_specs=[VMEM] * len(shapes),
        cost_estimate=pl.CostEstimate(flops=0, bytes_accessed=0, transcendentals=0),
        name=name,
    )(*args)


def pack_kernel(spot, gain, query, key, value, output, mine, theirs):
    rows = query.shape[0]
    part = query.shape[1] // 4
    row = lax.broadcasted_iota(jnp.int32, (rows, rows), 0)
    column = lax.broadcasted_iota(jnp.int32, (rows, rows), 1)
    spread = jnp.broadcast_to(gain[...].astype(F32), (rows, rows))
    scale = jnp.where(row == column, spread, 0.0).astype(BF)
    scaled = [plain(scale, w[...]).astype(BF) for w in (query, key, value)] + [output[...]]
    for low in range(2):
        classes = []
        for kind in (0, 2):
            pieces = []
            for core in range(2):
                place = slice((2 * low + core) * part, (2 * low + core + 1) * part)
                pieces += [scaled[kind][:, place], scaled[kind + 1][:, place]]
            classes.append(jnp.concatenate(pieces, axis=1))
        mine[low] = jnp.where(spot[0] == 0, classes[0], classes[1])
        theirs[low] = jnp.where(spot[0] == 0, classes[1], classes[0])


def cross_kernel(spot, mine, got, keep, send):
    first = [jnp.where(spot[0] == 0, mine[low], got[low]) for low in range(2)]
    second = [jnp.where(spot[0] == 0, got[low], mine[low]) for low in range(2)]
    for core, rows in enumerate((first, second)):
        keep[core] = jnp.where(spot[1] == 0, rows[0], rows[1])
        send[core] = jnp.where(spot[1] == 0, rows[1], rows[0])


def place_kernel(spot, keep, got, block):
    rows = keep.shape[1]
    for core in range(2):
        first = jnp.where(spot[1] == 0, keep[core], got[core])
        second = jnp.where(spot[1] == 0, got[core], keep[core])
        block[rows * core : rows * (core + 1), :] = first
        block[rows * (2 + core) : rows * (3 + core), :] = second


def exchange_cores(pieces):
    core = lax.axis_index("c")
    mine = jnp.where(core == 0, pieces[:, 0], pieces[:, 1])
    theirs = swap(jnp.where(core == 0, pieces[:, 1], pieces[:, 0]), "c")
    return jnp.stack(
        [jnp.where(core == 0, mine, theirs), jnp.where(core == 0, theirs, mine)], axis=1
    )


def exchange_chips(cores):
    low = lax.axis_index("l")
    mine = jnp.where(low == 0, cores[0], cores[1])
    theirs = swap(jnp.where(low == 0, cores[1], cores[0]), "l")
    return jnp.stack([jnp.where(low == 0, mine, theirs), jnp.where(low == 0, theirs, mine)], axis=0)


def exchange(pieces):
    return exchange_chips(exchange_cores(pieces))


def split_pieces(weight, width):
    rows, columns = weight.shape
    pieces = weight.reshape(rows, 4, columns // 4)
    return jnp.pad(pieces, ((0, 0), (0, 0), (0, width - columns // 4)))


def to_pieces(weights, widths):
    joined = jnp.concatenate([split_pieces(w, n) for w, n in zip(weights, widths)], axis=2)
    rows = joined.shape[0]
    return joined.transpose(1, 0, 2).reshape(2, 2, rows, joined.shape[2])


PLANE = ("y", "x", "c")


def along(values, distance, second):
    pairs = []
    for place in range(32):
        y, x, core = place // 8, place // 2 % 4, place % 2
        if (core == 0) != second:
            target = (y, (x + distance) % 4, core)
        else:
            target = ((y + distance) % 4, x, core)
        pairs.append((place, (target[0] * 4 + target[1]) * 2 + target[2]))
    return lax.ppermute(values, PLANE, pairs)


def gather_line(block):
    return jnp.stack([block] + [along(block, -d, False) for d in (1, 2, 3)])


def gather_plane(line):
    after1, after3 = along(line, -1, True), along(line, 1, True)
    return after1, after3


def gather_far_line(after1, after3):
    half = after1.shape[0] // 2
    return along(after1[:half], -1, True), along(after3[half:], 1, True)


def reduce_far(part):
    return along(part[:2], 1, False), along(part[2:], -1, False)


def reduce_near(part0, part1, part3, relayed1, relayed3):
    to1 = (part1[:2].astype(F32) + relayed1.astype(F32)).astype(BF)
    to3 = (part3[2:].astype(F32) + relayed3.astype(F32)).astype(BF)
    from1 = along(jnp.concatenate([to1, part1[2:]]), 1, False)
    from3 = along(jnp.concatenate([part3[:2], to3]), -1, False)
    return (part0.astype(F32) + from1.astype(F32) + from3.astype(F32)).astype(BF)


def reduce_line(line):
    total = line[0].astype(F32)
    for d in (1, 3, 2):
        total = total + along(line[d], d, True).astype(F32)
    return total


def rms_unit(rows):
    inv = lax.rsqrt(jnp.mean(rows * rows, axis=-1, keepdims=True) + EPSILON)
    return rows * inv, inv


def rms_back(grad_unit, unit, inv):
    return inv * (grad_unit - unit * jnp.mean(grad_unit * unit, axis=-1, keepdims=True))


def places(half):
    core = lax.axis_index("c")
    ring = lax.axis_index("t") * 2 + lax.axis_index("l")
    start = jnp.stack([ring // 2, ((ring + 3 - 2 * core) % 4) // 2]).astype(jnp.int32) * half
    length = 2 * half
    frequency = ROPE_BASE ** (-jnp.arange(HD // 2, dtype=F32) * 2.0 / HD)
    angles = jnp.arange(length, dtype=F32)[:, None] * frequency[None, :]
    cosine, sine = jnp.cos(angles), jnp.sin(angles)
    tables = []
    for i in range(2):
        for table in (jnp.concatenate([cosine] * 2, 1), jnp.concatenate([-sine, sine], 1)):
            tables.append(jnp.where(start[i] == 0, table, jnp.roll(table, half, axis=0)))
    spot = jnp.concatenate([start, jnp.stack([lax.axis_index(a) for a in ("c", "y", "x")])])
    return spot.astype(jnp.int32), tables[:2], tables[2:]


HBM = pl.BlockSpec(memory_space=pltpu.HBM)


LIMIT = pltpu.CompilerParams(vmem_limit_bytes=32 * 2**20)


def cost(us):
    return pl.CostEstimate(flops=int(us * 1.1e9), bytes_accessed=0, transcendentals=0)


def kernel_call(body, shapes, us, args, specs, scratch, name):
    return pl.pallas_call(
        body,
        out_shape=[jax.ShapeDtypeStruct(shape, BF) for shape in shapes],
        in_specs=specs,
        out_specs=[VMEM] * len(shapes),
        scratch_shapes=list(scratch),
        compiler_params=LIMIT,
        cost_estimate=cost(us),
        name=name,
    )(*args)


def wait_all(copies):
    for copy in copies:
        copy.wait()


def causal_mask(start, length):
    def place(dim):
        index = lax.broadcasted_iota(jnp.int32, (length, length), dim) + start
        return jnp.where(index >= length, index - length, index)

    return place(0) >= place(1)


def soft_weights(query, key, mask):
    scores = jnp.where(mask, times_t(query, key) * (1.0 / math.sqrt(HD)), MASKED)
    weights = jnp.exp(scores - jnp.max(scores, axis=-1, keepdims=True))
    return weights / jnp.sum(weights, axis=-1, keepdims=True)


def turned(values, cosine, sine):
    return values * cosine + pltpu.roll(values, HD // 2, 1) * sine


def fetch(pairs, sems, first=0):
    copies = [pltpu.make_async_copy(a, b, sems.at[first + i]) for i, (a, b) in enumerate(pairs)]
    for copy in copies:
        copy.start()
    return copies


def joined(blocks, target, first=0):
    rows = blocks[0].shape[0]
    return [
        (block, target.at[pl.ds(first + rows * n, rows), :]) for n, block in enumerate(blocks)
    ]


def feature_block(core, y, x, first, second):
    dy, dx = jnp.where(core == 0, second, first), jnp.where(core == 0, first, second)
    return lax.rem(y + dy, 4) * 4 + lax.rem(x + dx, 4)


def plane_blocks(spot, lines, target):
    core, y, x = spot[2], spot[3], spot[4]
    rows, size = lines[0].shape[1], lines[0].shape[2] // 2
    half = pl.ds(pl.multiple_of(core * size, size), size)
    pairs = []
    count = len(lines) // 2
    for kind, group in ((core, lines[:count]), (1 - core, lines[count:])):
        columns = pl.ds(pl.multiple_of(kind * size, size), size)
        for second in range(4):
            for first in range(4):
                row = pl.multiple_of(feature_block(kind, y, x, first, second) * rows, rows)
                if second == 2 and count == 5:
                    source = group[3 + first // 2].at[first % 2, :, half]
                else:
                    source = group[(0, 1, 3, 2)[second]].at[first, :, half]
                pairs.append((source, target.at[pl.ds(row, rows), columns]))
    return pairs


OUTS = {EVEN: ((0, 0), (0, 1), (1, 0), (1, 1)), ODD: ((1, 1), (0, 0), (1, 0), (0, 1))}


def product_t(left, weight, targets, slots, chunk):
    rows = left.shape[0] // 4

    def step(i, carry):
        part = pl.ds(pl.multiple_of(i * chunk, chunk), chunk)
        found = times_t(left[...], weight[part, :]).astype(BF)
        for n, (target, block) in enumerate(OUTS[slots]):
            place = slice(rows * block, rows * (block + 1))
            targets[target][place, part] = found[rows * n : rows * (n + 1)]
        return carry

    lax.fori_loop(0, weight.shape[0] // chunk, step, 0)


def norm_back_kernel(count, kinds, *refs):
    outs, staged, sems = refs[count + 2 : count + 2 + kinds], refs[count + 2 + kinds : -1], refs[-1]
    rows = staged[0].shape[0]
    starts = [rows if i == count - 1 and ref.shape[0] > rows else 0 for i, ref in enumerate(refs)]
    pairs = [
        (ref.at[pl.ds(start, rows), :], to)
        for ref, start, to in zip(refs[: count + 2], starts, staged)
    ]
    wait_all(fetch(pairs, sems))
    grad = sum(ref[...].astype(F32) for ref in staged[:count])
    unit, inv = rms_unit(staged[count][...].astype(F32))
    found = staged[count + 1][...].astype(F32) + rms_back(grad, unit, inv)
    for out in outs:
        out[...] = found.astype(out.dtype)


def norm_back(terms, rows, base, kinds):
    args = (*terms, rows, base)
    return pl.pallas_call(
        functools.partial(norm_back_kernel, len(terms), len(kinds)),
        out_shape=[jax.ShapeDtypeStruct(rows.shape, kind) for kind in kinds],
        in_specs=[HBM] * len(args),
        out_specs=[VMEM] * len(kinds),
        scratch_shapes=[pltpu.VMEM(rows.shape, a.dtype) for a in args]
        + [pltpu.SemaphoreType.DMA((len(args),))],
        compiler_params=pltpu.CompilerParams(vmem_limit_bytes=(60 if OPT["nb60"] else 32) * 2**20),
        cost_estimate=pl.CostEstimate(flops=0, bytes_accessed=0, transcendentals=0),
        name="norm_back",
    )(*args)


def attend_kernel(slots, spot, *refs):
    if slots is ODD:
        n = len(refs) - 9
        arrays, lines, (cosine, sine) = refs[:4], refs[4:n], refs[n : n + 2]
        qkv, heads_cat, kept, sent, weight, rows, sems = refs[n + 2 :]
        copies = plane_blocks(spot, lines, weight)
    else:
        arrays, (weight, cosine, sine) = refs[:4], refs[4:7]
        qkv, heads_cat, kept, sent, rows, sems = refs[7:]
        copies = []
    part = weight.shape[1] // 4
    length = cosine.shape[0]
    wait_all(fetch(joined(arrays, rows) + copies, sems))
    both = plain(rows[...], weight[:, : 3 * part])
    qkv[:, 2 * part :] = both[:, 2 * part :].astype(BF)
    mask = causal_mask(spot[0 if slots is EVEN else 1], length)
    for s in range(2):
        here = slice(s * length, (s + 1) * length)
        for i in range(part // HD):
            columns = slice(i * HD, (i + 1) * HD)
            others = slice(part + i * HD, part + (i + 1) * HD)
            values = slice(2 * part + i * HD, 2 * part + (i + 1) * HD)
            query = turned(both[here, columns], cosine[...], sine[...]).astype(BF)
            key = turned(both[here, others], cosine[...], sine[...]).astype(BF)
            qkv[here, columns] = query
            qkv[here, others] = key
            soft = soft_weights(query, key, mask).astype(BF)
            heads_cat[here, columns] = plain(soft, qkv[here, values]).astype(BF)
    product_t(heads_cat, weight.at[:, 3 * part :], (kept, sent), slots, 512)


def size_of(arrays):
    return sum(array.shape[0] for array in arrays), arrays[0].shape[1]


def attend(slots, spot, arrays, weights, tables):
    rows, width = size_of(arrays)
    odd = slots is ODD
    part = (weights[0] if odd else weights).shape[-1] // 4
    weights = list(weights) if odd else [weights]
    return kernel_call(
        functools.partial(attend_kernel, slots),
        [(rows, 3 * part), (rows, part), (rows // 2, width), (rows // 2, width)]
        + [(width, 4 * part)] * odd,
        OPT["ka_odd"] if odd else OPT["ka_even"],
        (spot, *arrays, *weights, *tables),
        [SMEM] + [HBM] * len(arrays) + [HBM if odd else VMEM] * len(weights) + [VMEM] * 2,
        [pltpu.VMEM((rows, width), BF), pltpu.SemaphoreType.DMA((36,))],
        name="attend",
    )


def attend_back_kernel(slots, spot, *refs):
    arrays, (weight, qkv_in, cosine, sine) = refs[:4], refs[4:8]
    grad_qkv, kept, sent, rows, qkv, sems = refs[8:]
    part = weight.shape[1] // 4
    length = cosine.shape[0]
    factor = 1.0 / math.sqrt(HD)
    wait_all(fetch(joined(arrays, rows) + [(qkv_in, qkv)], sems))
    grad_heads = plain(rows[...], weight[:, 3 * part :]).astype(BF)
    mask = causal_mask(spot[0 if slots is EVEN else 1], length)
    for s in range(2):
        here = slice(s * length, (s + 1) * length)
        for i in range(part // HD):
            columns = slice(i * HD, (i + 1) * HD)
            others = slice(part + i * HD, part + (i + 1) * HD)
            values = slice(2 * part + i * HD, 2 * part + (i + 1) * HD)
            query, key = qkv[here, columns], qkv[here, others]
            soft = soft_weights(query, key, mask)
            grad_mix = grad_heads[here, columns]
            grad_soft = times_t(grad_mix, qkv[here, values])
            grad_qkv[here, values] = left_t(soft.astype(BF), grad_mix).astype(BF)
            inner = jnp.sum(grad_soft * soft, axis=-1, keepdims=True)
            grad_scores = (soft * (grad_soft - inner)).astype(BF)
            back_q = plain(grad_scores, key) * factor
            back_k = left_t(grad_scores, query) * factor
            grad_qkv[here, columns] = turned(back_q, cosine[...], -sine[...]).astype(BF)
            grad_qkv[here, others] = turned(back_k, cosine[...], -sine[...]).astype(BF)
    product_t(grad_qkv, weight.at[:, : 3 * part], (kept, sent), slots, 512)


def attend_back(slots, spot, arrays, qkv, weight, tables):
    rows, width = size_of(arrays)
    part = weight.shape[1] // 4
    return kernel_call(
        functools.partial(attend_back_kernel, slots),
        [(rows, 3 * part), (rows // 2, width), (rows // 2, width)],
        OPT["kd_odd"] if slots is ODD else OPT["kd_even"],
        (spot, *arrays, weight, qkv, *tables),
        [SMEM] + [HBM] * 4 + [VMEM, HBM] + [VMEM] * 2,
        [pltpu.VMEM((rows, width), BF), pltpu.VMEM((rows, 3 * part), BF)]
        + [pltpu.SemaphoreType.DMA((5,))],
        name="attend_back",
    )


def sent_product_t(left, weight, staged, targets, slots, sems, first):
    rows, chunk = left.shape[0] // 4, weight.shape[0] // 4
    copies = []
    for i in range(4):
        part = pl.ds(i * chunk, chunk)
        staged[:, part] = times_t(left[...], weight[part, :]).astype(BF)
        pairs = [
            (
                staged.at[pl.ds(rows * n, rows), part],
                targets[target].at[pl.ds(rows * block, rows), part],
            )
            for n, (target, block) in enumerate(OUTS[slots])
        ]
        copies += fetch(pairs, sems, first + 4 * i)
    return copies


def feed_kernel(slots, *refs):
    arrays, gradients, source = refs[:4], refs[4:8], refs[8]
    activation_out, grad_gu_out, kept, sent, grad_kept, grad_sent = refs[9:15]
    activation, grad_gu, staged, grad_staged, rows, grads, weight, sems = refs[15:]
    wide = weight.shape[1] // 3
    chunk = min(256, wide)
    chunks = wide // chunk
    row_copies = fetch(joined(arrays, rows), sems)

    def part(kind, i):
        return pl.ds(wide * kind + chunk * i, chunk)

    def load(kind, i):
        columns = part(kind, i)
        return fetch([(source.at[:, columns], weight.at[:, columns])], sems, 8 + 3 * i + kind)

    gate_up_copies = [load(0, i) + load(1, i) for i in range(chunks)]
    grad_copies = fetch(joined(gradients, grads), sems, 4)
    down_copies = [load(2, i) for i in range(chunks)]
    wait_all(row_copies)
    found = []
    for i in range(chunks):
        wait_all(gate_up_copies[i])
        found.append([plain(rows[...], weight[:, part(kind, i)]) for kind in range(2)])
    wait_all(grad_copies)
    for copies in down_copies:
        wait_all(copies)
    for i in range(chunks):
        gate, up = found[i]
        grad_act = plain(grads[...], weight[:, part(2, i)])
        sigmoid = jax.nn.sigmoid(gate)
        swish = gate * sigmoid
        activation[:, part(0, i)] = (swish * up).astype(BF)
        grad_gate = grad_act * up * (sigmoid + swish * (1.0 - sigmoid))
        grad_gu[:, part(0, i)] = grad_gate.astype(BF)
        grad_gu[:, part(1, i)] = (grad_act * swish).astype(BF)
    copies = fetch([(activation, activation_out), (grad_gu, grad_gu_out)], sems)
    down, gate_up = weight.at[:, 2 * wide :], weight.at[:, : 2 * wide]
    copies += sent_product_t(activation, down, staged, (kept, sent), slots, sems, 2)
    copies += sent_product_t(
        grad_gu, gate_up, grad_staged, (grad_kept, grad_sent), slots, sems, 18
    )
    wait_all(copies)


def feed(slots, arrays, grads, weight):
    rows, width = size_of(arrays)
    wide = weight.shape[1] // 3
    shapes = [(rows, wide), (rows, 2 * wide)]
    scratch = shapes + [(rows, width)] * 4 + [(width, 3 * wide)]
    shapes = shapes + [(rows // 2, width)] * 4
    return pl.pallas_call(
        functools.partial(feed_kernel, slots),
        out_shape=[jax.ShapeDtypeStruct(shape, BF) for shape in shapes],
        in_specs=[HBM] * (2 * len(arrays) + 1),
        out_specs=[HBM] * len(shapes),
        scratch_shapes=[pltpu.VMEM(shape, BF) for shape in scratch]
        + [pltpu.SemaphoreType.DMA((34,))],
        compiler_params=pltpu.CompilerParams(vmem_limit_bytes=60 * 2**20),
        cost_estimate=cost(OPT["fd_odd"] if slots is ODD else OPT["fd_even"]),
        name="feed",
    )(*arrays, *grads, weight)


def feed_weights_kernel(start, *refs):
    out = refs[-5]
    rows, right, staged, sems = refs[-4:]
    middle = right.shape[0] // 2
    pairs = joined(refs[:8], rows)
    pairs += [(refs[8 + i], right.at[pl.ds(middle * i, middle), :]) for i in range(2)]
    wait_all(fetch(pairs, sems))
    tile, width = 256, right.shape[1]
    outs = []
    for i in range(rows.shape[1] // tile):
        part = pl.ds(tile * i, tile)
        staged[part, :] = left_t(rows[:, part], right[...]).astype(BF)
        place = out.at[part, pl.ds(start, width)]
        outs += fetch([(staged.at[part, :], place)], sems, 10 + i)
    wait_all(outs)


def feed_weights(blocks, rights, columns, start, us, onto=None):
    rows, width = blocks[0].shape
    right = rights[0].shape[1]
    args = (*blocks, *rights) + (() if onto is None else (onto,))
    return pl.pallas_call(
        functools.partial(feed_weights_kernel, start),
        out_shape=jax.ShapeDtypeStruct((width, columns), BF),
        in_specs=[HBM] * len(args),
        out_specs=HBM,
        scratch_shapes=[
            pltpu.VMEM((8 * rows, width), BF),
            pltpu.VMEM((8 * rows, right), BF),
            pltpu.VMEM((width, right), BF),
            pltpu.SemaphoreType.DMA((10 + width // 256,)),
        ],
        input_output_aliases={} if onto is None else {10: 0},
        compiler_params=pltpu.CompilerParams(vmem_limit_bytes=60 * 2**20),
        cost_estimate=cost(us),
        name="feed_weights",
    )(*args)


def attend_weights_kernel(spot, *refs):
    grads, heads = refs[16:18], refs[18:20]
    keeps, sends, (ins, hiddens, sems) = refs[20:24], refs[24:28], refs[28:]
    wait_all(fetch(joined(refs[:8], ins) + joined(refs[8:16], hiddens), sems))
    tile, size = keeps[0].shape[1:]

    def step(first, j):
        columns = []
        for second in (j, j + 1):
            block = feature_block(spot[2], spot[3], spot[4], first, second)
            columns.append(pl.ds(pl.multiple_of(block * tile, tile), tile))
        found = []
        for rows, rights in ((ins, grads), (hiddens, heads)):
            left = jnp.concatenate([rows[:, c] for c in columns], axis=1)
            right = jnp.concatenate([r[...] for r in rights], axis=0)
            found.append(left_t(left, right).astype(BF))
        both = jnp.concatenate(found, axis=1)
        left, right = both[:, :size], both[:, size:]
        kept = jnp.where(spot[2] == 0, left, right)
        sent = jnp.where(spot[2] == 0, right, left)
        for k in range(2):
            keeps[first][j + k] = kept[tile * k : tile * (k + 1)]
            sends[j + k][first] = sent[tile * k : tile * (k + 1)]

    for first in range(4):
        for j in (0, 2):
            step(first, j)


def attend_weights(spot, ins, hiddens, grads, heads):
    rows, width = ins[0].shape
    tile = width // 16
    size = (grads[0].shape[1] + heads[0].shape[1]) // 2
    found = kernel_call(
        attend_weights_kernel,
        [(4, tile, size)] * 8,
        OPT["ke"],
        (spot, *ins, *hiddens, *grads, *heads),
        [SMEM] + [HBM] * 16 + [VMEM] * 4,
        [pltpu.VMEM((8 * rows, width), BF)] * 2 + [pltpu.SemaphoreType.DMA((16,))],
        name="attend_weights",
    )
    return found[:4], found[4:]


def shards(
    layer_input,
    attn_scale,
    query_weight,
    key_weight,
    value_weight,
    output_weight,
    mlp_scale,
    gate_weight,
    up_weight,
    down_weight,
    out_grad,
):
    half, width = layer_input.shape
    gain_attn = attn_scale.astype(F32)[:, None]
    gain_mlp = mlp_scale.astype(F32)[:, None]
    part = query_weight.shape[1] // 4
    units = gate_weight.shape[1] // 4
    wide = -(-units // 128) * 128

    def scaled(weight, gain):
        return (weight.astype(F32) * gain).astype(BF)

    low_rows = query_weight.shape[0]
    attn_columns = [
        w.reshape(low_rows, 2, 2, part)
        for w in (
            scaled(query_weight, gain_attn),
            scaled(key_weight, gain_attn),
            scaled(value_weight, gain_attn),
            output_weight.T,
        )
    ]
    attn_pieces = jnp.stack(
        [jnp.concatenate(attn_columns[i : i + 2], axis=3) for i in (0, 2)], axis=1
    )
    attn_pieces = attn_pieces.reshape(low_rows, 2, 2, 4 * part).transpose(2, 1, 0, 3)
    mlp_pieces = to_pieces(
        [scaled(gate_weight, gain_mlp), scaled(up_weight, gain_mlp), down_weight.T], [wide] * 3
    )
    own_in = layer_input.astype(F32)
    unit_in, _ = rms_unit(own_in)
    own = unit_in.astype(BF)
    if OPT["pack"]:
        at = jnp.stack([lax.axis_index("c"), lax.axis_index("l")]).astype(jnp.int32)
        piece = jax.ShapeDtypeStruct((2, low_rows, 4 * part), BF)
        mine, theirs = small_call(
            pack_kernel,
            [piece] * 2,
            (at, attn_scale[None, :], query_weight, key_weight, value_weight, output_weight.T),
            "pack",
        )
        mine, theirs, own, other = stage(mine, swap(theirs, "c"), own, swap(own, "c"))
        kept, sent = small_call(cross_kernel, [piece] * 2, (at, mine, theirs), "cross")
        (attn_block,) = small_call(
            place_kernel,
            [jax.ShapeDtypeStruct((4 * low_rows, 4 * part), BF)],
            (at, kept, swap(sent, "l")),
            "place",
        )
    else:
        attn_cores, own, other = stage(exchange_cores(attn_pieces), own, swap(own, "c"))
        attn_block = exchange_chips(attn_cores).reshape(-1, 4 * part)
    attn_block, own, other, mlp_pieces = stage(attn_block, own, other, mlp_pieces)

    attn_line, p_mine = gather_line(attn_block), hop(own)
    mlp_cores = exchange_cores(mlp_pieces)
    if OPT["t2mlp"] == 1:
        attn_line, p_mine, other, mlp_cores, (spot, even_tables, odd_tables) = stage(
            attn_line, p_mine, other, mlp_cores, places(half)
        )
    else:
        attn_line, other, (spot, even_tables, odd_tables) = stage(
            attn_line, other, places(half)
        )
        if OPT["t2p"]:
            attn_line, p_mine, other = stage(attn_line, p_mine, other)

    near_lines, p_other = gather_plane(attn_line), hop(other)
    if OPT["t2mlp"] == 2:
        mlp_cores = after(mlp_cores, p_mine)
    mlp_block = exchange_chips(mlp_cores).reshape(-1, 3 * wide)
    swapped = [swap(attn_line, "c")]
    near_lines, p_other, mlp_block, p_mine, swapped = stage(
        near_lines, p_other, mlp_block, p_mine, swapped
    )

    mlp_weight = lax.all_gather(mlp_block, ("y", "x"), axis=0, tiled=True)
    far_lines, far = gather_far_line(*near_lines), hop(p_mine)
    swapped += [swap(v, "c") for v in near_lines]
    s_other, s_mine = swap(p_mine, "c"), swap(p_other, "c")
    if OPT["t4s"]:
        far_lines, far, swapped, s_other, s_mine = stage(far_lines, far, swapped, s_other, s_mine)
    else:
        far_lines, far = stage(far_lines, far)
    lines = [attn_line, *near_lines, *far_lines]
    lines += swapped + [swap(v, "c") for v in far_lines]
    odd_in = (p_mine, s_mine, p_other, s_other)

    odd_at = attend(ODD, spot, odd_in, lines, odd_tables)
    attn_weight = odd_at[4]
    far_other = swap(after(far, odd_at[0]) if OPT["ka_far"] else far, "c")
    even_in = (own, far, other, far_other)
    if OPT["g_after"] == "far":
        near_grad, odd_grad = gather_odd(out_grad, OPT["g_pair"], far)
    if OPT["g_after"] == "odd_at":
        near_grad, odd_grad = gather_odd(out_grad, OPT["g_pair"], attn_weight)
    even_in = after(even_in, attn_weight)
    if OPT["g_before"] == "even_at":
        even_in = after(even_in, odd_grad[0], odd_grad[2])
    even_at = attend(EVEN, spot, even_in, attn_weight, even_tables)
    even_sums = even_at[2:4]
    if OPT["g_before"] == "rs1":
        even_sums = after(even_sums, odd_grad[0], odd_grad[2])
    hidden = own_in + total(group_sum(even_sums, odd_at[2:4], OPT["rs1_early"]))

    unit_mid, _ = rms_unit(hidden)
    unit_mid = unit_mid.astype(BF)
    if OPT["g_before"] == "hidden":
        unit_mid = after(unit_mid, odd_grad[0], odd_grad[2])
    near_mid, odd_mid = gather_odd(unit_mid, OPT["m_pair"])
    odd_feed = feed(ODD, odd_mid, odd_grad, mlp_weight)
    ties = [odd_feed[0]] if OPT["feed_far"] else []
    even_mid = gather_far(near_mid, odd_mid, *ties)
    even_grad = gather_far(near_grad, odd_grad, *ties)
    even_feed = feed(EVEN, even_mid, even_grad, mlp_weight)
    gu_rights, down_rights = (even_feed[1], odd_feed[1]), (even_feed[0], odd_feed[0])
    rows_mid, rows_grad = even_mid + odd_mid, even_grad + odd_grad
    works = [(rows_mid, gu_rights, 0), (rows_grad, down_rights, 2 * wide)]
    if OPT["down_first"]:
        works = works[::-1]
    gu_first = feed_weights(*works[0][:2], 3 * wide, works[0][2], OPT["kca_us"])
    mlp_partial = feed_weights(*works[1][:2], 3 * wide, works[1][2], OPT["kcb_us"], gu_first)
    ties = {"r1": [gu_first], "r2": []}[OPT["kca_at"]]
    terms = group_sum(even_feed[4:], odd_feed[4:], OPT["rs2_early"], ties, mlp_partial)
    mlp_sum = lax.psum_scatter(
        after(mlp_partial, terms[-1] if OPT["rs_tie"] == "crossed" else terms[-2]),
        ("y", "x"),
        scatter_dimension=0,
        tiled=True,
    )
    if OPT["low"]:
        (low_hidden,) = norm_back(terms, hidden, out_grad, (BF,))
        grad_hidden = low_hidden
    else:
        grad_hidden, low_hidden = norm_back(terms, hidden, out_grad, (F32, BF))

    near_hidden, odd_hidden = gather_odd(low_hidden, OPT["h_pair"])
    odd_back = attend_back(ODD, spot, odd_hidden, odd_at[0], attn_weight, odd_tables)
    ties = [odd_back[0]] if OPT["kd_far"] else []
    even_hidden = gather_far(near_hidden, odd_hidden, *ties)
    even_back = attend_back(EVEN, spot, even_hidden, even_at[0], attn_weight, even_tables)
    got, side = swap(even_back[2], "c"), swap(odd_back[2], "c")
    keep, send = attend_weights(
        spot,
        even_in + odd_in,
        even_hidden + odd_hidden,
        (even_back[0], odd_back[0]),
        (even_at[1], odd_at[1]),
    )
    keep, send, got, side = stage(keep, send, got, side)

    def both(i):
        return jnp.concatenate([keep[i], swap(send[i], "c")], axis=-1)

    def finish(odd, side, relayed, cat):
        sums = near_sums(odd, side, relayed)
        if cat:
            last = hop(jnp.concatenate(sums))
            return last, swap(last, "c")
        mine, other = (hop(block) for block in sums)
        return mine, jnp.concatenate([mine, swap(other, "c")])

    relayed1, relayed3 = reduce_far(both(2))
    relayed = hop(far_sum(even_back[1:], got))
    out_even, out_odd = after((even_feed[2:4], odd_feed[2:4]), got)
    out_got, out_side = swap(out_even[1], "c"), swap(out_odd[1], "c")
    parts = both(0), both(1), both(3)
    relayed1, relayed3, relayed, parts, out_got, out_side = stage(
        relayed1, relayed3, relayed, parts, out_got, out_side
    )
    if OPT["u1out"]:
        out_relayed = hop(far_sum(out_even, out_got))
        relayed1, out_relayed = stage(relayed1, out_relayed)

    attn_line = reduce_near(*parts, relayed1, relayed3)
    last, crossed = finish(odd_back[1:], side, relayed, OPT["in_cat"])
    if not OPT["u1out"]:
        out_relayed = hop(far_sum(out_even, out_got))
    mlp_cores = exchange_cores(mlp_sum.reshape(2, 2, -1, 3 * wide))
    attn_line, last, crossed, mlp_cores = stage(attn_line, last, crossed, mlp_cores)
    if OPT["u2out"]:
        attn_line, out_relayed = stage(attn_line, out_relayed)

    attn_sum, mlp_own = reduce_line(attn_line), exchange_chips(mlp_cores)
    out_last, out_crossed = finish(out_odd, out_side, out_relayed, OPT["out_cat"])
    terms = (even_back[1], got, last, crossed)
    (input_grad,) = norm_back(terms, layer_input, grad_hidden, (BF,))
    if OPT["u3out"]:
        attn_sum, out_last = stage(attn_sum, out_last)
    if OPT["u3in"]:
        attn_sum, input_grad = stage(attn_sum, input_grad)
    if OPT["u3mlp"]:
        attn_sum, mlp_own = stage(attn_sum, mlp_own)
    out_terms = (out_even[0], out_got, out_last[:half], out_crossed[half:])
    layer_output = (hidden + total(out_terms)).astype(BF)

    def whole(pieces, start, size):
        piece = pieces[..., start : start + size].reshape(4, -1, size)
        return piece.transpose(1, 0, 2).reshape(-1, 4 * size).astype(F32)

    def gain_of(pairs):
        return sum(jnp.sum(w.astype(F32) * g, axis=1) for w, g in pairs)

    size = 2 * part
    core = lax.axis_index("c")
    attn_sum = jnp.where(core == 0, attn_sum, jnp.roll(attn_sum, size, axis=1)).astype(BF)
    attn_cores = exchange_cores(attn_sum.reshape(2, 2, -1, 2 * size))
    gate_own, up_own, down_own = (whole(mlp_own, wide * i, units) for i in range(3))
    gate_grad, up_grad = gate_own * gain_mlp, up_own * gain_mlp
    mlp_gain = gain_of([(gate_weight, gate_own), (up_weight, up_own)])
    if OPT["u4mlp"]:
        attn_cores, gate_grad, up_grad, down_own, mlp_gain = stage(
            attn_cores, gate_grad, up_grad, down_own, mlp_gain
        )
    attn_own = exchange_chips(attn_cores)
    if OPT["u4mlp"] == 2:
        attn_own, gate_grad, up_grad, down_own, mlp_gain, layer_output = stage(
            attn_own, gate_grad, up_grad, down_own, mlp_gain, layer_output
        )

    def attn_whole(kind, start):
        piece = attn_own[:, kind].reshape(2, low_rows, 2, size)[..., start : start + part]
        return piece.transpose(1, 0, 2, 3).reshape(low_rows, 4 * part).astype(F32)

    query_own, key_own, value_own, output_own = (
        attn_whole(kind, start) for kind in (0, 1) for start in (0, part)
    )
    gains = jnp.stack(
        [
            gain_of([(query_weight, query_own), (key_weight, key_own), (value_weight, value_own)]),
            mlp_gain,
        ]
    )
    attn_gain, mlp_gain = gains + swap(gains, "t")
    return (
        layer_output,
        input_grad,
        attn_gain,
        query_own * gain_attn,
        key_own * gain_attn,
        value_own * gain_attn,
        output_own.T,
        mlp_gain,
        gate_grad,
        up_grad,
        down_own.T,
    )


def solution(mesh):
    devices = mesh.devices.reshape(4, 4, 2, 2, 2)
    fine = Mesh(devices, ("y", "x", "l", "c", "t"))
    rows = P(GROUP + ("t",), None)
    gain, into, out = P(GROUP), P(GROUP, "t"), P("t", GROUP)
    return jax.shard_map(
        shards,
        mesh=fine,
        in_specs=(rows, gain, into, into, into, out, gain, into, into, out, rows),
        out_specs=(rows, rows, gain, into, into, into, out, gain, into, into, out),
        check_vma=False,
    )
```

```python
import functools
import math

import jax
import jax.numpy as jnp
from jax import lax
from jax.experimental import pallas as pl
from jax.experimental.pallas import tpu as pltpu
from jax.sharding import Mesh, PartitionSpec as P

HD = 128
EPSILON = 1e-05
ROPE_BASE = 10000.0
MASKED = -1e30
BF = jnp.bfloat16
F32 = jnp.float32

GROUP = ("y", "x", "l", "c")
RING = ("l", "c", "t")


def plain(left, right):
    return jnp.dot(left, right, preferred_element_type=F32)


def times_t(left, right):
    return lax.dot_general(left, right, (((1,), (1,)), ((), ())), preferred_element_type=F32)


def left_t(left, right):
    return lax.dot_general(left, right, (((0,), (0,)), ((), ())), preferred_element_type=F32)


def swap(values, axis):
    return lax.ppermute(values, axis, [(0, 1), (1, 0)])


def hop(values):
    def place(z, core):
        return (z % 2) * 4 + core * 2 + z // 2

    pairs = []
    for z in range(4):
        pairs.append((place(z, 0), place((z + 1) % 4, 0)))
        pairs.append((place(z, 1), place((z + 3) % 4, 1)))
    return lax.ppermute(values, RING, pairs)


def after(values, *others):
    return lax.optimization_barrier((values, *others))[0]


def stage(*values):
    return lax.optimization_barrier(values)


EVEN, ODD = "even", "odd"


def gather_odd(rows):
    other = swap(rows, "c")
    p_mine, p_other = hop(rows), hop(other)
    return (rows, other), (p_mine, swap(p_other, "c"), p_other, swap(p_mine, "c"))


def gather_far(near, odd, *others):
    far = hop(after(odd[0], odd[1], odd[3]))
    return (near[0], far, near[1], swap(after(far, *others), "c"))


def far_sum(even, got):
    rows = got.shape[0] // 2
    return (even[0][rows:].astype(F32) + got[rows:].astype(F32)).astype(BF)


def near_sums(odd, side, relayed):
    rows = relayed.shape[0]
    mine = odd[0][:rows].astype(F32) + side[:rows].astype(F32) + relayed.astype(F32)
    other = odd[0][rows:].astype(F32) + side[rows:].astype(F32)
    return mine.astype(BF), other.astype(BF)


def fold(even, got):
    rows = got.shape[0] // 2
    own = even[0][:rows].astype(F32) + got[:rows].astype(F32)
    return stage(far_sum(even, got), own)


def relayed_sum(even, odd):
    rows = even[0].shape[0] // 2
    side = swap(odd[1], "c")
    other = hop((odd[0][rows:].astype(F32) + side[rows:].astype(F32)).astype(BF))
    far, own = fold(even, swap(even[1], "c"))
    relayed = hop(far)
    mine = odd[0][:rows].astype(F32) + side[:rows].astype(F32) + relayed.astype(F32)
    return own, hop(mine.astype(BF)), swap(other, "c")


def direct_sum(even, odd, side_after, *others):
    side = swap(after(odd[1], *side_after), "c")
    pair = hop((odd[0].astype(F32) + side.astype(F32)).astype(BF))
    far, own = fold(even, swap(even[1], "c"))
    terms = swap(far, "t"), pair, swap(pair, "c")
    far, pair, crossed = after(terms, *others)
    return own, pair, far, crossed


def total(terms):
    rows = terms[-2].shape[0]
    last = terms[-1][-rows:]
    return sum(term[:rows].astype(F32) for term in terms[:-1]) + last.astype(F32)


VMEM = pl.BlockSpec(memory_space=pltpu.VMEM)
SMEM = pl.BlockSpec(memory_space=pltpu.SMEM)


def exchange_cores(pieces):
    core = lax.axis_index("c")
    mine = jnp.where(core == 0, pieces[:, 0], pieces[:, 1])
    theirs = swap(jnp.where(core == 0, pieces[:, 1], pieces[:, 0]), "c")
    return jnp.stack(
        [jnp.where(core == 0, mine, theirs), jnp.where(core == 0, theirs, mine)], axis=1
    )


def exchange_chips(cores):
    low = lax.axis_index("l")
    mine = jnp.where(low == 0, cores[0], cores[1])
    theirs = swap(jnp.where(low == 0, cores[1], cores[0]), "l")
    return jnp.stack([jnp.where(low == 0, mine, theirs), jnp.where(low == 0, theirs, mine)], axis=0)


def split_pieces(weight, width):
    rows, columns = weight.shape
    pieces = weight.reshape(rows, 4, columns // 4)
    return jnp.pad(pieces, ((0, 0), (0, 0), (0, width - columns // 4)))


def to_pieces(weights, widths):
    joined = jnp.concatenate([split_pieces(w, n) for w, n in zip(weights, widths)], axis=2)
    rows = joined.shape[0]
    return joined.transpose(1, 0, 2).reshape(2, 2, rows, joined.shape[2])


PLANE = ("y", "x", "c")


def along(values, distance, second):
    pairs = []
    for place in range(32):
        y, x, core = place // 8, place // 2 % 4, place % 2
        if (core == 0) != second:
            target = (y, (x + distance) % 4, core)
        else:
            target = ((y + distance) % 4, x, core)
        pairs.append((place, (target[0] * 4 + target[1]) * 2 + target[2]))
    return lax.ppermute(values, PLANE, pairs)


def gather_line(block):
    return jnp.stack([block] + [along(block, -d, False) for d in (1, 2, 3)])


def gather_plane(line):
    return along(line, -1, True), along(line, 1, True)


def gather_far_line(after1, after3):
    half = after1.shape[0] // 2
    return along(after1[:half], -1, True), along(after3[half:], 1, True)


def reduce_far(part):
    return along(part[:2], 1, False), along(part[2:], -1, False)


def near_operands(part1, part3, relayed1, relayed3):
    to1 = (part1[:2].astype(F32) + relayed1.astype(F32)).astype(BF)
    to3 = (part3[2:].astype(F32) + relayed3.astype(F32)).astype(BF)
    return jnp.concatenate([to1, part1[2:]]), jnp.concatenate([part3[:2], to3])


def reduce_near(part0, to1, to3):
    from1, from3 = along(to1, 1, False), along(to3, -1, False)
    return (part0.astype(F32) + from1.astype(F32) + from3.astype(F32)).astype(BF)


def reduce_line(line):
    total = line[0].astype(F32)
    for d in (1, 3, 2):
        total = total + along(line[d], d, True).astype(F32)
    return total


def rms_unit(rows):
    inv = lax.rsqrt(jnp.mean(rows * rows, axis=-1, keepdims=True) + EPSILON)
    return rows * inv, inv


def rms_back(grad_unit, unit, inv):
    return inv * (grad_unit - unit * jnp.mean(grad_unit * unit, axis=-1, keepdims=True))


def places(half):
    core = lax.axis_index("c")
    ring = lax.axis_index("t") * 2 + lax.axis_index("l")
    start = jnp.stack([ring // 2, ((ring + 3 - 2 * core) % 4) // 2]).astype(jnp.int32) * half
    length = 2 * half
    frequency = ROPE_BASE ** (-jnp.arange(HD // 2, dtype=F32) * 2.0 / HD)
    angles = jnp.arange(length, dtype=F32)[:, None] * frequency[None, :]
    cosine, sine = jnp.cos(angles), jnp.sin(angles)
    tables = []
    for i in range(2):
        for table in (jnp.concatenate([cosine] * 2, 1), jnp.concatenate([-sine, sine], 1)):
            tables.append(jnp.where(start[i] == 0, table, jnp.roll(table, half, axis=0)))
    spot = jnp.concatenate([start, jnp.stack([lax.axis_index(a) for a in ("c", "y", "x")])])
    return spot.astype(jnp.int32), tables[:2], tables[2:]


HBM = pl.BlockSpec(memory_space=pltpu.HBM)


LIMIT = pltpu.CompilerParams(vmem_limit_bytes=32 * 2**20)


def cost(us):
    return pl.CostEstimate(flops=int(us * 1.1e9), bytes_accessed=0, transcendentals=0)


def kernel_call(body, shapes, us, args, specs, scratch, name):
    return pl.pallas_call(
        body,
        out_shape=[jax.ShapeDtypeStruct(shape, BF) for shape in shapes],
        in_specs=specs,
        out_specs=[VMEM] * len(shapes),
        scratch_shapes=list(scratch),
        compiler_params=LIMIT,
        cost_estimate=cost(us),
        name=name,
    )(*args)


def wait_all(copies):
    for copy in copies:
        copy.wait()


def causal_mask(start, length):
    def place(dim):
        index = lax.broadcasted_iota(jnp.int32, (length, length), dim) + start
        return jnp.where(index >= length, index - length, index)

    return place(0) >= place(1)


def soft_weights(query, key, mask):
    scores = jnp.where(mask, times_t(query, key) * (1.0 / math.sqrt(HD)), MASKED)
    weights = jnp.exp(scores - jnp.max(scores, axis=-1, keepdims=True))
    return weights / jnp.sum(weights, axis=-1, keepdims=True)


def turned(values, cosine, sine):
    return values * cosine + pltpu.roll(values, HD // 2, 1) * sine


def fetch(pairs, sems, first=0):
    copies = [pltpu.make_async_copy(a, b, sems.at[first + i]) for i, (a, b) in enumerate(pairs)]
    for copy in copies:
        copy.start()
    return copies


def joined(blocks, target, first=0):
    rows = blocks[0].shape[0]
    return [
        (block, target.at[pl.ds(first + rows * n, rows), :]) for n, block in enumerate(blocks)
    ]


def feature_block(core, y, x, first, second):
    dy, dx = jnp.where(core == 0, second, first), jnp.where(core == 0, first, second)
    return lax.rem(y + dy, 4) * 4 + lax.rem(x + dx, 4)


def plane_blocks(spot, lines, target):
    core, y, x = spot[2], spot[3], spot[4]
    rows, size = lines[0].shape[1], lines[0].shape[2] // 2
    half = pl.ds(pl.multiple_of(core * size, size), size)
    pairs = []
    for kind, group in ((core, lines[:5]), (1 - core, lines[5:])):
        columns = pl.ds(pl.multiple_of(kind * size, size), size)
        for second in range(4):
            for first in range(4):
                row = pl.multiple_of(feature_block(kind, y, x, first, second) * rows, rows)
                if second == 2:
                    source = group[3 + first // 2].at[first % 2, :, half]
                else:
                    source = group[(0, 1, None, 2)[second]].at[first, :, half]
                pairs.append((source, target.at[pl.ds(row, rows), columns]))
    return pairs


OUTS = {EVEN: ((0, 0), (0, 1), (1, 0), (1, 1)), ODD: ((1, 1), (0, 0), (1, 0), (0, 1))}


def product_t(left, weight, targets, slots, chunk):
    rows = left.shape[0] // 4

    def step(i, carry):
        part = pl.ds(pl.multiple_of(i * chunk, chunk), chunk)
        found = times_t(left[...], weight[part, :]).astype(BF)
        for n, (target, block) in enumerate(OUTS[slots]):
            place = slice(rows * block, rows * (block + 1))
            targets[target][place, part] = found[rows * n : rows * (n + 1)]
        return carry

    lax.fori_loop(0, weight.shape[0] // chunk, step, 0)


def norm_back_kernel(count, *refs):
    staged, sems = refs[count + 3 : -1], refs[-1]
    rows = staged[0].shape[0]
    starts = [0] * count + [0, 0]
    starts[count - 1] = refs[count - 1].shape[0] - rows
    pairs = [(ref.at[pl.ds(first, rows), :], to) for ref, first, to in zip(refs, starts, staged)]
    wait_all(fetch(pairs, sems))
    grad = sum(ref[...].astype(F32) for ref in staged[:count])
    unit, inv = rms_unit(staged[count][...].astype(F32))
    base = staged[count + 1][...].astype(F32)
    refs[count + 2][...] = (base + rms_back(grad, unit, inv)).astype(BF)


def norm_back(terms, rows, base):
    args = (*terms, rows, base)
    return pl.pallas_call(
        functools.partial(norm_back_kernel, len(terms)),
        out_shape=jax.ShapeDtypeStruct(rows.shape, BF),
        in_specs=[HBM] * len(args),
        out_specs=VMEM,
        scratch_shapes=[pltpu.VMEM(rows.shape, a.dtype) for a in args]
        + [pltpu.SemaphoreType.DMA((len(args),))],
        compiler_params=pltpu.CompilerParams(vmem_limit_bytes=60 * 2**20),
        cost_estimate=cost(0),
        name="norm_back",
    )(*args)


def attend_kernel(slots, spot, *refs):
    if slots is ODD:
        n = len(refs) - 9
        arrays, lines, (cosine, sine) = refs[:4], refs[4:n], refs[n : n + 2]
        qkv, heads_cat, kept, sent, weight, rows, sems = refs[n + 2 :]
        copies = plane_blocks(spot, lines, weight)
    else:
        arrays, (weight, cosine, sine) = refs[:4], refs[4:7]
        qkv, heads_cat, kept, sent, rows, sems = refs[7:]
        copies = []
    part = weight.shape[1] // 4
    length = cosine.shape[0]
    wait_all(fetch(joined(arrays, rows) + copies, sems))
    both = plain(rows[...], weight[:, : 3 * part])
    qkv[:, 2 * part :] = both[:, 2 * part :].astype(BF)
    mask = causal_mask(spot[0 if slots is EVEN else 1], length)
    for s in range(2):
        here = slice(s * length, (s + 1) * length)
        for i in range(part // HD):
            columns = slice(i * HD, (i + 1) * HD)
            others = slice(part + i * HD, part + (i + 1) * HD)
            values = slice(2 * part + i * HD, 2 * part + (i + 1) * HD)
            query = turned(both[here, columns], cosine[...], sine[...]).astype(BF)
            key = turned(both[here, others], cosine[...], sine[...]).astype(BF)
            qkv[here, columns] = query
            qkv[here, others] = key
            soft = soft_weights(query, key, mask).astype(BF)
            heads_cat[here, columns] = plain(soft, qkv[here, values]).astype(BF)
    product_t(heads_cat, weight.at[:, 3 * part :], (kept, sent), slots, 512)


def size_of(arrays):
    return sum(array.shape[0] for array in arrays), arrays[0].shape[1]


def attend(slots, spot, arrays, weights, tables):
    rows, width = size_of(arrays)
    odd = slots is ODD
    part = (weights[0] if odd else weights).shape[-1] // 4
    weights = list(weights) if odd else [weights]
    return kernel_call(
        functools.partial(attend_kernel, slots),
        [(rows, 3 * part), (rows, part), (rows // 2, width), (rows // 2, width)]
        + [(width, 4 * part)] * odd,
        0 if odd else 2,
        (spot, *arrays, *weights, *tables),
        [SMEM] + [HBM] * len(arrays) + [HBM if odd else VMEM] * len(weights) + [VMEM] * 2,
        [pltpu.VMEM((rows, width), BF), pltpu.SemaphoreType.DMA((36,))],
        name="attend",
    )


def attend_back_kernel(slots, spot, *refs):
    arrays, (weight, qkv_in, cosine, sine) = refs[:4], refs[4:8]
    grad_qkv, kept, sent, rows, qkv, sems = refs[8:]
    part = weight.shape[1] // 4
    length = cosine.shape[0]
    factor = 1.0 / math.sqrt(HD)
    wait_all(fetch(joined(arrays, rows) + [(qkv_in, qkv)], sems))
    grad_heads = plain(rows[...], weight[:, 3 * part :]).astype(BF)
    mask = causal_mask(spot[0 if slots is EVEN else 1], length)
    for s in range(2):
        here = slice(s * length, (s + 1) * length)
        for i in range(part // HD):
            columns = slice(i * HD, (i + 1) * HD)
            others = slice(part + i * HD, part + (i + 1) * HD)
            values = slice(2 * part + i * HD, 2 * part + (i + 1) * HD)
            query, key = qkv[here, columns], qkv[here, others]
            soft = soft_weights(query, key, mask)
            grad_mix = grad_heads[here, columns]
            grad_soft = times_t(grad_mix, qkv[here, values])
            grad_qkv[here, values] = left_t(soft.astype(BF), grad_mix).astype(BF)
            inner = jnp.sum(grad_soft * soft, axis=-1, keepdims=True)
            grad_scores = (soft * (grad_soft - inner)).astype(BF)
            back_q = plain(grad_scores, key) * factor
            back_k = left_t(grad_scores, query) * factor
            grad_qkv[here, columns] = turned(back_q, cosine[...], -sine[...]).astype(BF)
            grad_qkv[here, others] = turned(back_k, cosine[...], -sine[...]).astype(BF)
    product_t(grad_qkv, weight.at[:, : 3 * part], (kept, sent), slots, 512)


def attend_back(slots, spot, arrays, qkv, weight, tables):
    rows, width = size_of(arrays)
    part = weight.shape[1] // 4
    return kernel_call(
        functools.partial(attend_back_kernel, slots),
        [(rows, 3 * part), (rows // 2, width), (rows // 2, width)],
        0,
        (spot, *arrays, weight, qkv, *tables),
        [SMEM] + [HBM] * 4 + [VMEM, HBM] + [VMEM] * 2,
        [pltpu.VMEM((rows, width), BF), pltpu.VMEM((rows, 3 * part), BF)]
        + [pltpu.SemaphoreType.DMA((5,))],
        name="attend_back",
    )


def sent_product_t(left, weight, staged, targets, slots, sems, first):
    rows, chunk = left.shape[0] // 4, weight.shape[0] // 4
    copies = []
    for i in range(4):
        part = pl.ds(i * chunk, chunk)
        staged[:, part] = times_t(left[...], weight[part, :]).astype(BF)
        pairs = [
            (
                staged.at[pl.ds(rows * n, rows), part],
                targets[target].at[pl.ds(rows * block, rows), part],
            )
            for n, (target, block) in enumerate(OUTS[slots])
        ]
        copies += fetch(pairs, sems, first + 4 * i)
    return copies


def feed_kernel(slots, units, *refs):
    arrays, gradients, source = refs[:4], refs[4:8], refs[8]
    activation_out, grad_gu_out, kept, sent, grad_kept, grad_sent = refs[9:15]
    activation, grad_gu, compact, staged, grad_staged, rows, grads, weight, sems = refs[15:]
    wide = weight.shape[1] // 3
    chunk = min(256, wide)
    chunks = wide // chunk
    row_copies = fetch(joined(arrays, rows), sems)

    def part(kind, i):
        return pl.ds(wide * kind + chunk * i, chunk)

    def load(kind, i):
        columns = part(kind, i)
        return fetch([(source.at[:, columns], weight.at[:, columns])], sems, 8 + 3 * i + kind)

    gate_up_copies = [load(0, i) + load(1, i) for i in range(chunks)]
    grad_copies = fetch(joined(gradients, grads), sems, 4)
    down_copies = [load(2, i) for i in range(chunks)]
    wait_all(row_copies)
    found = []
    for i in range(chunks):
        wait_all(gate_up_copies[i])
        found.append([plain(rows[...], weight[:, part(kind, i)]) for kind in range(2)])
    wait_all(grad_copies)
    for copies in down_copies:
        wait_all(copies)
    for i in range(chunks):
        gate, up = found[i]
        grad_act = plain(grads[...], weight[:, part(2, i)])
        sigmoid = jax.nn.sigmoid(gate)
        swish = gate * sigmoid
        activation[:, part(0, i)] = (swish * up).astype(BF)
        grad_gate = grad_act * up * (sigmoid + swish * (1.0 - sigmoid))
        grad_gu[:, part(0, i)] = grad_gate.astype(BF)
        grad_gu[:, part(1, i)] = (grad_act * swish).astype(BF)
    compact[:, :units] = grad_gu[:, :units]
    compact[:, units : 2 * units] = grad_gu[:, wide : wide + units]
    compact[:, 2 * units :] = jnp.zeros_like(compact[:, 2 * units :])
    copies = fetch([(activation, activation_out), (compact, grad_gu_out)], sems)
    down, gate_up = weight.at[:, 2 * wide :], weight.at[:, : 2 * wide]
    copies += sent_product_t(activation, down, staged, (kept, sent), slots, sems, 2)
    copies += sent_product_t(
        grad_gu, gate_up, grad_staged, (grad_kept, grad_sent), slots, sems, 18
    )
    wait_all(copies)


def together(units):
    return -(-2 * units // 128) * 128


def feed(slots, arrays, grads, weight, units):
    rows, width = size_of(arrays)
    wide = weight.shape[1] // 3
    shapes = [(rows, wide), (rows, together(units))]
    scratch = [(rows, wide), (rows, 2 * wide), shapes[1]]
    scratch += [(rows, width)] * 4 + [(width, 3 * wide)]
    shapes += [(rows // 2, width)] * 4
    return pl.pallas_call(
        functools.partial(feed_kernel, slots, units),
        out_shape=[jax.ShapeDtypeStruct(shape, BF) for shape in shapes],
        in_specs=[HBM] * (2 * len(arrays) + 1),
        out_specs=[HBM] * len(shapes),
        scratch_shapes=[pltpu.VMEM(shape, BF) for shape in scratch]
        + [pltpu.SemaphoreType.DMA((34,))],
        compiler_params=pltpu.CompilerParams(vmem_limit_bytes=60 * 2**20),
        cost_estimate=cost(0 if slots is ODD else 8),
        name="feed",
    )(*arrays, *grads, weight)


def feed_weights_kernel(start, *refs):
    grad_gus, activations, out = refs[16:18], refs[18:20], refs[20]
    rows, grads, grad_gu, activation, staged, sems = refs[21:]
    middle = grad_gu.shape[0] // 2

    def pair(halves, target):
        return [(half, target.at[pl.ds(middle * i, middle), :]) for i, half in enumerate(halves)]

    first = fetch(joined(refs[:8], rows) + pair(grad_gus, grad_gu), sems)
    second = fetch(joined(refs[8:16], grads) + pair(activations, activation), sems, 10)
    wait_all(first)
    tile = 256
    outs = []
    for i in range(rows.shape[1] // tile):
        part = pl.ds(tile * i, tile)
        staged[part, :start] = left_t(rows[:, part], grad_gu[...]).astype(BF)
        if i == 0:
            wait_all(second)
        staged[part, start:] = left_t(grads[:, part], activation[...]).astype(BF)
        outs += fetch([(staged.at[part, :], out.at[part, :])], sems, 20 + i)
    wait_all(outs)


def feed_weights(rows, grads, grad_gus, activations, us):
    count, width = rows[0].shape
    sizes = [grad_gus[0].shape[1], activations[0].shape[1]]
    args = (*rows, *grads, *grad_gus, *activations)
    shapes = [(8 * count, width)] * 2 + [(8 * count, n) for n in sizes] + [(width, sum(sizes))]
    return pl.pallas_call(
        functools.partial(feed_weights_kernel, sizes[0]),
        out_shape=jax.ShapeDtypeStruct((width, sum(sizes)), BF),
        in_specs=[HBM] * len(args),
        out_specs=HBM,
        scratch_shapes=[pltpu.VMEM(shape, BF) for shape in shapes]
        + [pltpu.SemaphoreType.DMA((20 + width // 256,))],
        compiler_params=pltpu.CompilerParams(vmem_limit_bytes=60 * 2**20),
        cost_estimate=cost(us),
        name="feed_weights",
    )(*args)


def attend_weights_kernel(spot, *refs):
    grads, heads = refs[16:18], refs[18:20]
    keeps, sends, (ins, hiddens, sems) = refs[20:24], refs[24:28], refs[28:]
    wait_all(fetch(joined(refs[:8], ins) + joined(refs[8:16], hiddens), sems))
    tile, size = keeps[0].shape[1:]

    def step(first, j):
        columns = []
        for second in (j, j + 1):
            block = feature_block(spot[2], spot[3], spot[4], first, second)
            columns.append(pl.ds(pl.multiple_of(block * tile, tile), tile))
        found = []
        for rows, rights in ((ins, grads), (hiddens, heads)):
            left = jnp.concatenate([rows[:, c] for c in columns], axis=1)
            right = jnp.concatenate([r[...] for r in rights], axis=0)
            found.append(left_t(left, right).astype(BF))
        both = jnp.concatenate(found, axis=1)
        left, right = both[:, :size], both[:, size:]
        kept = jnp.where(spot[2] == 0, left, right)
        sent = jnp.where(spot[2] == 0, right, left)
        for k in range(2):
            keeps[first][j + k] = kept[tile * k : tile * (k + 1)]
            sends[j + k][first] = sent[tile * k : tile * (k + 1)]

    for first in range(4):
        for j in (0, 2):
            step(first, j)


def attend_weights(spot, ins, hiddens, grads, heads):
    rows, width = ins[0].shape
    tile = width // 16
    size = (grads[0].shape[1] + heads[0].shape[1]) // 2
    found = kernel_call(
        attend_weights_kernel,
        [(4, tile, size)] * 8,
        0,
        (spot, *ins, *hiddens, *grads, *heads),
        [SMEM] + [HBM] * 16 + [VMEM] * 4,
        [pltpu.VMEM((8 * rows, width), BF)] * 2 + [pltpu.SemaphoreType.DMA((16,))],
        name="attend_weights",
    )
    return found[:4], found[4:]


def shards(
    layer_input,
    attn_scale,
    query_weight,
    key_weight,
    value_weight,
    output_weight,
    mlp_scale,
    gate_weight,
    up_weight,
    down_weight,
    out_grad,
):
    half, width = layer_input.shape
    gain_attn = attn_scale.astype(F32)[:, None]
    gain_mlp = mlp_scale.astype(F32)[:, None]
    part = query_weight.shape[1] // 4
    units = gate_weight.shape[1] // 4
    wide = -(-units // 128) * 128

    def scaled(weight, gain):
        return (weight.astype(F32) * gain).astype(BF)

    low_rows = query_weight.shape[0]
    attn_columns = [
        w.reshape(low_rows, 2, 2, part)
        for w in (
            scaled(query_weight, gain_attn),
            scaled(key_weight, gain_attn),
            scaled(value_weight, gain_attn),
            output_weight.T,
        )
    ]
    attn_pieces = jnp.stack(
        [jnp.concatenate(attn_columns[i : i + 2], axis=3) for i in (0, 2)], axis=1
    )
    attn_pieces = attn_pieces.reshape(low_rows, 2, 2, 4 * part).transpose(2, 1, 0, 3)
    mlp_pieces = to_pieces(
        [scaled(gate_weight, gain_mlp), scaled(up_weight, gain_mlp), down_weight.T], [wide] * 3
    )
    own_in = layer_input.astype(F32)
    own = rms_unit(own_in)[0].astype(BF)

    attn_cores, own, other = stage(exchange_cores(attn_pieces), own, swap(own, "c"))

    attn_block = exchange_chips(attn_cores).reshape(-1, 4 * part)
    attn_block, own, other, mlp_pieces = stage(attn_block, own, other, mlp_pieces)

    attn_line, p_mine = gather_line(attn_block), hop(own)
    mlp_cores = exchange_cores(mlp_pieces)
    attn_line, p_mine, other, (spot, even_tables, odd_tables) = stage(
        attn_line, p_mine, other, places(half)
    )

    near_lines, p_other = gather_plane(attn_line), hop(other)
    mlp_block = exchange_chips(after(mlp_cores, p_mine)).reshape(-1, 3 * wide)
    swapped = [swap(attn_line, "c")]
    near_lines, p_other, mlp_block, p_mine, swapped = stage(
        near_lines, p_other, mlp_block, p_mine, swapped
    )

    mlp_weight = lax.all_gather(mlp_block, ("y", "x"), axis=0, tiled=True)
    far_lines, far = gather_far_line(*near_lines), hop(p_mine)
    swapped += [swap(v, "c") for v in near_lines]
    odd_in = (p_mine, swap(p_other, "c"), p_other, swap(p_mine, "c"))
    far_lines, far = stage(far_lines, far)

    grad_mine, other_grad = hop(after(out_grad, p_other)), swap(out_grad, "c")
    grad_other = hop(after(other_grad, far))
    near_grad = (out_grad, other_grad)
    odd_grad = (grad_mine, swap(grad_other, "c"), grad_other, swap(grad_mine, "c"))

    lines = (attn_line, *near_lines, *far_lines, *swapped, *(swap(v, "c") for v in far_lines))
    odd_at = attend(ODD, spot, odd_in, lines, odd_tables)
    attn_weight = odd_at[4]
    even_in = after((own, far, other, swap(far, "c")), attn_weight)
    even_at = attend(EVEN, spot, even_in, attn_weight, even_tables)
    even_sums = after(even_at[2:4], grad_mine, grad_other)
    hidden = own_in + total(relayed_sum(even_sums, odd_at[2:4]))

    near_mid, odd_mid = gather_odd(rms_unit(hidden)[0].astype(BF))
    odd_feed = feed(ODD, odd_mid, odd_grad, mlp_weight, units)
    even_mid = gather_far(near_mid, odd_mid, odd_feed[0])
    even_grad = gather_far(near_grad, odd_grad, odd_feed[0])
    even_feed = feed(EVEN, even_mid, even_grad, mlp_weight, units)
    mlp_partial = feed_weights(
        even_mid + odd_mid,
        even_grad + odd_grad,
        (even_feed[1], odd_feed[1]),
        (even_feed[0], odd_feed[0]),
        3,
    )
    terms = direct_sum(even_feed[4:], odd_feed[4:], (even_mid[1], even_grad[1]), mlp_partial)
    mlp_sum = lax.psum_scatter(
        after(mlp_partial, terms[2]), ("y", "x"), scatter_dimension=0, tiled=True
    )
    grad_hidden = norm_back(terms, hidden, out_grad)

    near_hidden, odd_hidden = gather_odd(grad_hidden)
    odd_back = attend_back(ODD, spot, odd_hidden, odd_at[0], attn_weight, odd_tables)
    even_hidden = gather_far(near_hidden, odd_hidden, odd_back[0])
    even_back = attend_back(EVEN, spot, even_hidden, even_at[0], attn_weight, even_tables)
    got, side = swap(even_back[2], "c"), swap(odd_back[2], "c")
    keep, send = attend_weights(
        spot,
        even_in + odd_in,
        even_hidden + odd_hidden,
        (even_back[0], odd_back[0]),
        (even_at[1], odd_at[1]),
    )
    keep, send, got, side = stage(keep, send, got, side)

    def both(i):
        return jnp.concatenate([keep[i], swap(send[i], "c")], axis=-1)

    def finish(odd, side, relayed):
        last = hop(jnp.concatenate(near_sums(odd, side, relayed)))
        return last, swap(last, "c")

    relayed1, relayed3 = reduce_far(both(2))
    relayed = hop(far_sum(even_back[1:], got))
    out_even, out_odd = after((even_feed[2:4], odd_feed[2:4]), got)
    out_got, out_side = swap(out_even[1], "c"), swap(out_odd[1], "c")
    parts = both(0), both(1), both(3)
    relayed1, relayed3, relayed, parts, out_got, out_side = stage(
        relayed1, relayed3, relayed, parts, out_got, out_side
    )

    attn_line = reduce_near(parts[0], *near_operands(*parts[1:], relayed1, relayed3))
    last, crossed = finish(odd_back[1:], side, relayed)
    out_relayed = hop(far_sum(out_even, out_got))
    mlp_cores = exchange_cores(mlp_sum.reshape(2, 2, -1, mlp_sum.shape[1]))
    attn_line, last, crossed, mlp_cores = stage(attn_line, last, crossed, mlp_cores)

    attn_sum, mlp_own = reduce_line(attn_line), exchange_chips(mlp_cores)
    out_last, out_crossed = finish(out_odd, out_side, out_relayed)
    input_grad = norm_back((even_back[1], got, last, crossed), layer_input, grad_hidden)
    attn_sum, mlp_own, input_grad = stage(attn_sum, mlp_own, input_grad)
    layer_output = (hidden + total((out_even[0], out_got, out_last[:half], out_crossed))).astype(BF)

    def whole(pieces, start, size):
        piece = pieces[..., start : start + size].reshape(4, -1, size)
        return piece.transpose(1, 0, 2).reshape(-1, 4 * size).astype(F32)

    def gain_of(pairs):
        return sum(jnp.sum(w.astype(F32) * g, axis=1) for w, g in pairs)

    size = 2 * part
    core = lax.axis_index("c")
    attn_sum = jnp.where(core == 0, attn_sum, jnp.roll(attn_sum, size, axis=1)).astype(BF)
    attn_cores = exchange_cores(attn_sum.reshape(2, 2, -1, 2 * size))
    starts = (0, units, together(units))
    gate_own, up_own, down_own = (whole(mlp_own, start, units) for start in starts)
    gate_grad, up_grad = gate_own * gain_mlp, up_own * gain_mlp
    mlp_gain = gain_of([(gate_weight, gate_own), (up_weight, up_own)])
    attn_cores, gate_grad, up_grad, down_own, mlp_gain = stage(
        attn_cores, gate_grad, up_grad, down_own, mlp_gain
    )
    attn_own = exchange_chips(attn_cores)

    def attn_whole(kind, start):
        piece = attn_own[:, kind].reshape(2, low_rows, 2, size)[..., start : start + part]
        return piece.transpose(1, 0, 2, 3).reshape(low_rows, 4 * part).astype(F32)

    query_own, key_own, value_own, output_own = (
        attn_whole(kind, start) for kind in (0, 1) for start in (0, part)
    )
    gains = jnp.stack(
        [
            gain_of([(query_weight, query_own), (key_weight, key_own), (value_weight, value_own)]),
            mlp_gain,
        ]
    )
    attn_gain, mlp_gain = gains + swap(gains, "t")
    return (
        layer_output,
        input_grad,
        attn_gain,
        query_own * gain_attn,
        key_own * gain_attn,
        value_own * gain_attn,
        output_own.T,
        mlp_gain,
        gate_grad,
        up_grad,
        down_own.T,
    )


def solution(mesh):
    devices = mesh.devices.reshape(4, 4, 2, 2, 2)
    fine = Mesh(devices, ("y", "x", "l", "c", "t"))
    rows = P(GROUP + ("t",), None)
    gain, into, out = P(GROUP), P(GROUP, "t"), P("t", GROUP)
    return jax.shard_map(
        shards,
        mesh=fine,
        in_specs=(rows, gain, into, into, into, out, gain, into, into, out, rows),
        out_specs=(rows, rows, gain, into, into, into, out, gain, into, into, out),
        check_vma=False,
    )
```

```python
import functools
import math

import jax
import jax.numpy as jnp
from jax import lax
from jax.experimental import pallas as pl
from jax.experimental.pallas import tpu as pltpu
from jax.sharding import Mesh, PartitionSpec as P

HD = 128
EPSILON = 1e-05
ROPE_BASE = 10000.0
MASKED = -1e30
BF = jnp.bfloat16
F32 = jnp.float32

GROUP = ("y", "x", "l", "c")
RING = ("l", "c", "t")


def plain(left, right):
    return jnp.dot(left, right, preferred_element_type=F32)


def times_t(left, right):
    return lax.dot_general(left, right, (((1,), (1,)), ((), ())), preferred_element_type=F32)


def left_t(left, right):
    return lax.dot_general(left, right, (((0,), (0,)), ((), ())), preferred_element_type=F32)


def swap(values, axis):
    return lax.ppermute(values, axis, [(0, 1), (1, 0)])


def hop(values):
    def place(z, core):
        return (z % 2) * 4 + core * 2 + z // 2

    pairs = []
    for z in range(4):
        pairs.append((place(z, 0), place((z + 1) % 4, 0)))
        pairs.append((place(z, 1), place((z + 3) % 4, 1)))
    return lax.ppermute(values, RING, pairs)


def after(values, *others):
    return lax.optimization_barrier((values, *others))[0]


def stage(*values):
    return lax.optimization_barrier(values)


EVEN, ODD = "even", "odd"


def gather_odd(rows):
    other = swap(rows, "c")
    p_mine, p_other = hop(rows), hop(other)
    return (rows, other), (p_mine, swap(p_other, "c"), p_other, swap(p_mine, "c"))


def gather_far(near, odd, *others):
    far = hop(after(odd[0], odd[1], odd[3]))
    return (near[0], far, near[1], swap(after(far, *others), "c"))


def far_sum(even, got):
    rows = got.shape[0] // 2
    return (even[0][rows:].astype(F32) + got[rows:].astype(F32)).astype(BF)


def near_sums(odd, side, relayed):
    rows = relayed.shape[0]
    mine = odd[0][:rows].astype(F32) + side[:rows].astype(F32) + relayed.astype(F32)
    other = odd[0][rows:].astype(F32) + side[rows:].astype(F32)
    return mine.astype(BF), other.astype(BF)


def fold(even, got):
    rows = got.shape[0] // 2
    own = even[0][:rows].astype(F32) + got[:rows].astype(F32)
    return stage(far_sum(even, got), own)


def relayed_sum(even, odd):
    rows = even[0].shape[0] // 2
    side = swap(odd[1], "c")
    other = hop((odd[0][rows:].astype(F32) + side[rows:].astype(F32)).astype(BF))
    far, own = fold(even, swap(even[1], "c"))
    relayed = hop(far)
    mine = odd[0][:rows].astype(F32) + side[:rows].astype(F32) + relayed.astype(F32)
    return own, hop(mine.astype(BF)), swap(other, "c")


def direct_sum(even, odd, side_after, *others):
    side = swap(after(odd[1], *side_after), "c")
    pair = hop((odd[0].astype(F32) + side.astype(F32)).astype(BF))
    got = swap(even[1], "c")
    terms = swap(far_sum(even, got), "t"), pair, swap(pair, "c")
    far, pair, crossed = after(terms, *others)
    return even[0], got, pair, far, crossed


def total(terms):
    rows = terms[-2].shape[0]
    last = terms[-1][-rows:]
    return sum(term[:rows].astype(F32) for term in terms[:-1]) + last.astype(F32)


VMEM = pl.BlockSpec(memory_space=pltpu.VMEM)
SMEM = pl.BlockSpec(memory_space=pltpu.SMEM)


def exchange_cores(pieces):
    core = lax.axis_index("c")
    mine = jnp.where(core == 0, pieces[:, 0], pieces[:, 1])
    theirs = swap(jnp.where(core == 0, pieces[:, 1], pieces[:, 0]), "c")
    return jnp.stack(
        [jnp.where(core == 0, mine, theirs), jnp.where(core == 0, theirs, mine)], axis=1
    )


def exchange_chips(cores):
    low = lax.axis_index("l")
    mine = jnp.where(low == 0, cores[0], cores[1])
    theirs = swap(jnp.where(low == 0, cores[1], cores[0]), "l")
    return jnp.stack([jnp.where(low == 0, mine, theirs), jnp.where(low == 0, theirs, mine)], axis=0)


def split_pieces(weight, width):
    rows, columns = weight.shape
    pieces = weight.reshape(rows, 4, columns // 4)
    return jnp.pad(pieces, ((0, 0), (0, 0), (0, width - columns // 4)))


def to_pieces(weights, widths):
    joined = jnp.concatenate([split_pieces(w, n) for w, n in zip(weights, widths)], axis=2)
    rows = joined.shape[0]
    return joined.transpose(1, 0, 2).reshape(2, 2, rows, joined.shape[2])


PLANE = ("y", "x", "c")


def along(values, distance, second):
    pairs = []
    for place in range(32):
        y, x, core = place // 8, place // 2 % 4, place % 2
        if (core == 0) != second:
            target = (y, (x + distance) % 4, core)
        else:
            target = ((y + distance) % 4, x, core)
        pairs.append((place, (target[0] * 4 + target[1]) * 2 + target[2]))
    return lax.ppermute(values, PLANE, pairs)


def gather_line(block):
    return jnp.stack([block] + [along(block, -d, False) for d in (1, 2, 3)])


def gather_plane(line):
    return along(line, -1, True), along(line, 1, True)


def gather_far_line(after1, after3):
    half = after1.shape[0] // 2
    return along(after1[:half], -1, True), along(after3[half:], 1, True)


def reduce_far(part):
    return along(part[:2], 1, False), along(part[2:], -1, False)


def near_operands(part1, part3, relayed1, relayed3):
    to1 = (part1[:2].astype(F32) + relayed1.astype(F32)).astype(BF)
    to3 = (part3[2:].astype(F32) + relayed3.astype(F32)).astype(BF)
    return jnp.concatenate([to1, part1[2:]]), jnp.concatenate([part3[:2], to3])


def reduce_near(part0, to1, to3):
    from1, from3 = along(to1, 1, False), along(to3, -1, False)
    return (part0.astype(F32) + from1.astype(F32) + from3.astype(F32)).astype(BF)


def reduce_line(line):
    total = line[0].astype(F32)
    for d in (1, 3, 2):
        total = total + along(line[d], d, True).astype(F32)
    return total


def rms_unit(rows):
    inv = lax.rsqrt(jnp.mean(rows * rows, axis=-1, keepdims=True) + EPSILON)
    return rows * inv, inv


def rms_back(grad_unit, unit, inv):
    return inv * (grad_unit - unit * jnp.mean(grad_unit * unit, axis=-1, keepdims=True))


def places(half):
    core = lax.axis_index("c")
    ring = lax.axis_index("t") * 2 + lax.axis_index("l")
    start = jnp.stack([ring // 2, ((ring + 3 - 2 * core) % 4) // 2]).astype(jnp.int32) * half
    length = 2 * half
    frequency = ROPE_BASE ** (-jnp.arange(HD // 2, dtype=F32) * 2.0 / HD)
    angles = jnp.arange(length, dtype=F32)[:, None] * frequency[None, :]
    cosine, sine = jnp.cos(angles), jnp.sin(angles)
    tables = []
    for i in range(2):
        for table in (jnp.concatenate([cosine] * 2, 1), jnp.concatenate([-sine, sine], 1)):
            tables.append(jnp.where(start[i] == 0, table, jnp.roll(table, half, axis=0)))
    spot = jnp.concatenate([start, jnp.stack([lax.axis_index(a) for a in ("c", "y", "x")])])
    return spot.astype(jnp.int32), tables[:2], tables[2:]


HBM = pl.BlockSpec(memory_space=pltpu.HBM)


LIMIT = pltpu.CompilerParams(vmem_limit_bytes=32 * 2**20)


def cost(us):
    return pl.CostEstimate(flops=int(us * 1.1e9), bytes_accessed=0, transcendentals=0)


def kernel_call(body, shapes, us, args, specs, scratch, name):
    return pl.pallas_call(
        body,
        out_shape=[jax.ShapeDtypeStruct(shape, BF) for shape in shapes],
        in_specs=specs,
        out_specs=[VMEM] * len(shapes),
        scratch_shapes=list(scratch),
        compiler_params=LIMIT,
        cost_estimate=cost(us),
        name=name,
    )(*args)


def wait_all(copies):
    for copy in copies:
        copy.wait()


def causal_mask(start, length):
    def place(dim):
        index = lax.broadcasted_iota(jnp.int32, (length, length), dim) + start
        return jnp.where(index >= length, index - length, index)

    return place(0) >= place(1)


def soft_weights(query, key, mask):
    scores = jnp.where(mask, times_t(query, key) * (1.0 / math.sqrt(HD)), MASKED)
    weights = jnp.exp(scores - jnp.max(scores, axis=-1, keepdims=True))
    return weights / jnp.sum(weights, axis=-1, keepdims=True)


def turned(values, cosine, sine):
    return values * cosine + pltpu.roll(values, HD // 2, 1) * sine


def fetch(pairs, sems, first=0):
    copies = [pltpu.make_async_copy(a, b, sems.at[first + i]) for i, (a, b) in enumerate(pairs)]
    for copy in copies:
        copy.start()
    return copies


def joined(blocks, target, first=0):
    rows = blocks[0].shape[0]
    return [
        (block, target.at[pl.ds(first + rows * n, rows), :]) for n, block in enumerate(blocks)
    ]


def feature_block(core, y, x, first, second):
    dy, dx = jnp.where(core == 0, second, first), jnp.where(core == 0, first, second)
    return lax.rem(y + dy, 4) * 4 + lax.rem(x + dx, 4)


def plane_blocks(spot, lines, target):
    core, y, x = spot[2], spot[3], spot[4]
    rows, size = lines[0].shape[1], lines[0].shape[2] // 2
    half = pl.ds(pl.multiple_of(core * size, size), size)
    pairs = []
    for kind, group in ((core, lines[:5]), (1 - core, lines[5:])):
        columns = pl.ds(pl.multiple_of(kind * size, size), size)
        for second in range(4):
            for first in range(4):
                row = pl.multiple_of(feature_block(kind, y, x, first, second) * rows, rows)
                if second == 2:
                    source = group[3 + first // 2].at[first % 2, :, half]
                else:
                    source = group[(0, 1, None, 2)[second]].at[first, :, half]
                pairs.append((source, target.at[pl.ds(row, rows), columns]))
    return pairs


OUTS = {EVEN: ((0, 0), (0, 1), (1, 0), (1, 1)), ODD: ((1, 1), (0, 0), (1, 0), (0, 1))}


def product_t(left, weight, targets, slots, chunk):
    rows = left.shape[0] // 4

    def step(i, carry):
        part = pl.ds(pl.multiple_of(i * chunk, chunk), chunk)
        found = times_t(left[...], weight[part, :]).astype(BF)
        for n, (target, block) in enumerate(OUTS[slots]):
            place = slice(rows * block, rows * (block + 1))
            targets[target][place, part] = found[rows * n : rows * (n + 1)]
        return carry

    lax.fori_loop(0, weight.shape[0] // chunk, step, 0)


def norm_back_kernel(count, *refs):
    staged, sems = refs[count + 3 : -1], refs[-1]
    rows = staged[0].shape[0]
    starts = [0] * count + [0, 0]
    starts[count - 1] = refs[count - 1].shape[0] - rows
    pairs = [(ref.at[pl.ds(first, rows), :], to) for ref, first, to in zip(refs, starts, staged)]
    wait_all(fetch(pairs, sems))
    grad = sum(ref[...].astype(F32) for ref in staged[:count])
    unit, inv = rms_unit(staged[count][...].astype(F32))
    base = staged[count + 1][...].astype(F32)
    refs[count + 2][...] = (base + rms_back(grad, unit, inv)).astype(BF)


def norm_back(terms, rows, base):
    args = (*terms, rows, base)
    return pl.pallas_call(
        functools.partial(norm_back_kernel, len(terms)),
        out_shape=jax.ShapeDtypeStruct(rows.shape, BF),
        in_specs=[HBM] * len(args),
        out_specs=VMEM,
        scratch_shapes=[pltpu.VMEM(rows.shape, a.dtype) for a in args]
        + [pltpu.SemaphoreType.DMA((len(args),))],
        compiler_params=pltpu.CompilerParams(vmem_limit_bytes=60 * 2**20),
        cost_estimate=cost(0),
        name="norm_back",
    )(*args)


def attend_kernel(slots, spot, *refs):
    if slots is ODD:
        n = len(refs) - 9
        arrays, lines, (cosine, sine) = refs[:4], refs[4:n], refs[n : n + 2]
        qkv, heads_cat, kept, sent, weight, rows, sems = refs[n + 2 :]
        copies = plane_blocks(spot, lines, weight)
    else:
        arrays, (weight, cosine, sine) = refs[:4], refs[4:7]
        qkv, heads_cat, kept, sent, rows, sems = refs[7:]
        copies = []
    part = weight.shape[1] // 4
    length = cosine.shape[0]
    wait_all(fetch(joined(arrays, rows) + copies, sems))
    both = plain(rows[...], weight[:, : 3 * part])
    qkv[:, 2 * part :] = both[:, 2 * part :].astype(BF)
    mask = causal_mask(spot[0 if slots is EVEN else 1], length)
    for s in range(2):
        here = slice(s * length, (s + 1) * length)
        for i in range(part // HD):
            columns = slice(i * HD, (i + 1) * HD)
            others = slice(part + i * HD, part + (i + 1) * HD)
            values = slice(2 * part + i * HD, 2 * part + (i + 1) * HD)
            query = turned(both[here, columns], cosine[...], sine[...]).astype(BF)
            key = turned(both[here, others], cosine[...], sine[...]).astype(BF)
            qkv[here, columns] = query
            qkv[here, others] = key
            soft = soft_weights(query, key, mask).astype(BF)
            heads_cat[here, columns] = plain(soft, qkv[here, values]).astype(BF)
    product_t(heads_cat, weight.at[:, 3 * part :], (kept, sent), slots, 512)


def size_of(arrays):
    return sum(array.shape[0] for array in arrays), arrays[0].shape[1]


def attend(slots, spot, arrays, weights, tables):
    rows, width = size_of(arrays)
    odd = slots is ODD
    part = (weights[0] if odd else weights).shape[-1] // 4
    weights = list(weights) if odd else [weights]
    return kernel_call(
        functools.partial(attend_kernel, slots),
        [(rows, 3 * part), (rows, part), (rows // 2, width), (rows // 2, width)]
        + [(width, 4 * part)] * odd,
        0 if odd else 2,
        (spot, *arrays, *weights, *tables),
        [SMEM] + [HBM] * len(arrays) + [HBM if odd else VMEM] * len(weights) + [VMEM] * 2,
        [pltpu.VMEM((rows, width), BF), pltpu.SemaphoreType.DMA((36,))],
        name="attend",
    )


def attend_back_kernel(slots, spot, *refs):
    arrays, (weight, qkv_in, cosine, sine) = refs[:4], refs[4:8]
    grad_qkv, kept, sent, rows, qkv, sems = refs[8:]
    part = weight.shape[1] // 4
    length = cosine.shape[0]
    factor = 1.0 / math.sqrt(HD)
    wait_all(fetch(joined(arrays, rows) + [(qkv_in, qkv)], sems))
    grad_heads = plain(rows[...], weight[:, 3 * part :]).astype(BF)
    mask = causal_mask(spot[0 if slots is EVEN else 1], length)
    for s in range(2):
        here = slice(s * length, (s + 1) * length)
        for i in range(part // HD):
            columns = slice(i * HD, (i + 1) * HD)
            others = slice(part + i * HD, part + (i + 1) * HD)
            values = slice(2 * part + i * HD, 2 * part + (i + 1) * HD)
            query, key = qkv[here, columns], qkv[here, others]
            soft = soft_weights(query, key, mask)
            grad_mix = grad_heads[here, columns]
            grad_soft = times_t(grad_mix, qkv[here, values])
            grad_qkv[here, values] = left_t(soft.astype(BF), grad_mix).astype(BF)
            inner = jnp.sum(grad_soft * soft, axis=-1, keepdims=True)
            grad_scores = (soft * (grad_soft - inner)).astype(BF)
            back_q = plain(grad_scores, key) * factor
            back_k = left_t(grad_scores, query) * factor
            grad_qkv[here, columns] = turned(back_q, cosine[...], -sine[...]).astype(BF)
            grad_qkv[here, others] = turned(back_k, cosine[...], -sine[...]).astype(BF)
    product_t(grad_qkv, weight.at[:, : 3 * part], (kept, sent), slots, 512)


def attend_back(slots, spot, arrays, qkv, weight, tables):
    rows, width = size_of(arrays)
    part = weight.shape[1] // 4
    return kernel_call(
        functools.partial(attend_back_kernel, slots),
        [(rows, 3 * part), (rows // 2, width), (rows // 2, width)],
        0,
        (spot, *arrays, weight, qkv, *tables),
        [SMEM] + [HBM] * 4 + [VMEM, HBM] + [VMEM] * 2,
        [pltpu.VMEM((rows, width), BF), pltpu.VMEM((rows, 3 * part), BF)]
        + [pltpu.SemaphoreType.DMA((5,))],
        name="attend_back",
    )


def sent_product_t(left, weight, staged, targets, slots, sems, first):
    rows, chunk = left.shape[0] // 4, weight.shape[0] // 4
    copies = []
    for i in range(4):
        part = pl.ds(i * chunk, chunk)
        staged[:, part] = times_t(left[...], weight[part, :]).astype(BF)
        pairs = [
            (
                staged.at[pl.ds(rows * n, rows), part],
                targets[target].at[pl.ds(rows * block, rows), part],
            )
            for n, (target, block) in enumerate(OUTS[slots])
        ]
        copies += fetch(pairs, sems, first + 4 * i)
    return copies


def feed_kernel(slots, units, *refs):
    arrays, gradients, source = refs[:4], refs[4:8], refs[8]
    activation_out, grad_gu_out, kept, sent, grad_kept, grad_sent = refs[9:15]
    activation, grad_gu, compact, staged, grad_staged, rows, grads, weight, sems = refs[15:]
    wide = weight.shape[1] // 3
    chunk = min(256, wide)
    chunks = wide // chunk
    row_copies = fetch(joined(arrays, rows), sems)

    def part(kind, i):
        return pl.ds(wide * kind + chunk * i, chunk)

    def load(kind, i):
        columns = part(kind, i)
        return fetch([(source.at[:, columns], weight.at[:, columns])], sems, 8 + 3 * i + kind)

    gate_up_copies = [load(0, i) + load(1, i) for i in range(chunks)]
    grad_copies = fetch(joined(gradients, grads), sems, 4)
    down_copies = [load(2, i) for i in range(chunks)]
    wait_all(row_copies)
    found = []
    for i in range(chunks):
        wait_all(gate_up_copies[i])
        found.append([plain(rows[...], weight[:, part(kind, i)]) for kind in range(2)])
    wait_all(grad_copies)
    for copies in down_copies:
        wait_all(copies)
    for i in range(chunks):
        gate, up = found[i]
        grad_act = plain(grads[...], weight[:, part(2, i)])
        sigmoid = jax.nn.sigmoid(gate)
        swish = gate * sigmoid
        activation[:, part(0, i)] = (swish * up).astype(BF)
        grad_gate = grad_act * up * (sigmoid + swish * (1.0 - sigmoid))
        grad_gu[:, part(0, i)] = grad_gate.astype(BF)
        grad_gu[:, part(1, i)] = (grad_act * swish).astype(BF)
    compact[:, :units] = grad_gu[:, :units]
    compact[:, units : 2 * units] = grad_gu[:, wide : wide + units]
    compact[:, 2 * units :] = jnp.zeros_like(compact[:, 2 * units :])
    copies = fetch([(activation, activation_out), (compact, grad_gu_out)], sems)
    down, gate_up = weight.at[:, 2 * wide :], weight.at[:, : 2 * wide]
    copies += sent_product_t(activation, down, staged, (kept, sent), slots, sems, 2)
    copies += sent_product_t(
        grad_gu, gate_up, grad_staged, (grad_kept, grad_sent), slots, sems, 18
    )
    wait_all(copies)


def together(units):
    return -(-2 * units // 128) * 128


def feed(slots, arrays, grads, weight, units):
    rows, width = size_of(arrays)
    wide = weight.shape[1] // 3
    shapes = [(rows, wide), (rows, together(units))]
    scratch = [(rows, wide), (rows, 2 * wide), shapes[1]]
    scratch += [(rows, width)] * 4 + [(width, 3 * wide)]
    shapes += [(rows // 2, width)] * 4
    return pl.pallas_call(
        functools.partial(feed_kernel, slots, units),
        out_shape=[jax.ShapeDtypeStruct(shape, BF) for shape in shapes],
        in_specs=[HBM] * (2 * len(arrays) + 1),
        out_specs=[HBM] * len(shapes),
        scratch_shapes=[pltpu.VMEM(shape, BF) for shape in scratch]
        + [pltpu.SemaphoreType.DMA((34,))],
        compiler_params=pltpu.CompilerParams(vmem_limit_bytes=60 * 2**20),
        cost_estimate=cost(0 if slots is ODD else 8),
        name="feed",
    )(*arrays, *grads, weight)


def feed_weights_kernel(start, *refs):
    grad_gus, activations, out = refs[16:18], refs[18:20], refs[20]
    rows, grads, grad_gu, activation, staged, sems = refs[21:]
    middle = grad_gu.shape[0] // 2

    def pair(halves, target):
        return [(half, target.at[pl.ds(middle * i, middle), :]) for i, half in enumerate(halves)]

    first = fetch(joined(refs[:8], rows) + pair(grad_gus, grad_gu), sems)
    second = fetch(joined(refs[8:16], grads) + pair(activations, activation), sems, 10)
    wait_all(first)
    tile = 256
    outs = []
    for i in range(rows.shape[1] // tile):
        part = pl.ds(tile * i, tile)
        staged[part, :start] = left_t(rows[:, part], grad_gu[...]).astype(BF)
        if i == 0:
            wait_all(second)
        staged[part, start:] = left_t(grads[:, part], activation[...]).astype(BF)
        outs += fetch([(staged.at[part, :], out.at[part, :])], sems, 20 + i)
    wait_all(outs)


def feed_weights(rows, grads, grad_gus, activations, us):
    count, width = rows[0].shape
    sizes = [grad_gus[0].shape[1], activations[0].shape[1]]
    args = (*rows, *grads, *grad_gus, *activations)
    shapes = [(8 * count, width)] * 2 + [(8 * count, n) for n in sizes] + [(width, sum(sizes))]
    return pl.pallas_call(
        functools.partial(feed_weights_kernel, sizes[0]),
        out_shape=jax.ShapeDtypeStruct((width, sum(sizes)), BF),
        in_specs=[HBM] * len(args),
        out_specs=HBM,
        scratch_shapes=[pltpu.VMEM(shape, BF) for shape in shapes]
        + [pltpu.SemaphoreType.DMA((20 + width // 256,))],
        compiler_params=pltpu.CompilerParams(vmem_limit_bytes=60 * 2**20),
        cost_estimate=cost(us),
        name="feed_weights",
    )(*args)


def attend_weights_kernel(spot, *refs):
    grads, heads = refs[16:18], refs[18:20]
    keeps, sends, (ins, hiddens, sems) = refs[20:24], refs[24:28], refs[28:]
    wait_all(fetch(joined(refs[:8], ins) + joined(refs[8:16], hiddens), sems))
    tile, size = keeps[0].shape[1:]

    def step(first, j):
        columns = []
        for second in (j, j + 1):
            block = feature_block(spot[2], spot[3], spot[4], first, second)
            columns.append(pl.ds(pl.multiple_of(block * tile, tile), tile))
        found = []
        for rows, rights in ((ins, grads), (hiddens, heads)):
            left = jnp.concatenate([rows[:, c] for c in columns], axis=1)
            right = jnp.concatenate([r[...] for r in rights], axis=0)
            found.append(left_t(left, right).astype(BF))
        both = jnp.concatenate(found, axis=1)
        left, right = both[:, :size], both[:, size:]
        kept = jnp.where(spot[2] == 0, left, right)
        sent = jnp.where(spot[2] == 0, right, left)
        for k in range(2):
            keeps[first][j + k] = kept[tile * k : tile * (k + 1)]
            sends[j + k][first] = sent[tile * k : tile * (k + 1)]

    for first in range(4):
        for j in (0, 2):
            step(first, j)


def attend_weights(spot, ins, hiddens, grads, heads):
    rows, width = ins[0].shape
    tile = width // 16
    size = (grads[0].shape[1] + heads[0].shape[1]) // 2
    found = kernel_call(
        attend_weights_kernel,
        [(4, tile, size)] * 8,
        0,
        (spot, *ins, *hiddens, *grads, *heads),
        [SMEM] + [HBM] * 16 + [VMEM] * 4,
        [pltpu.VMEM((8 * rows, width), BF)] * 2 + [pltpu.SemaphoreType.DMA((16,))],
        name="attend_weights",
    )
    return found[:4], found[4:]


def shards(
    layer_input,
    attn_scale,
    query_weight,
    key_weight,
    value_weight,
    output_weight,
    mlp_scale,
    gate_weight,
    up_weight,
    down_weight,
    out_grad,
):
    half, width = layer_input.shape
    gain_attn = attn_scale.astype(F32)[:, None]
    gain_mlp = mlp_scale.astype(F32)[:, None]
    part = query_weight.shape[1] // 4
    units = gate_weight.shape[1] // 4
    wide = -(-units // 128) * 128

    def scaled(weight, gain):
        return (weight.astype(F32) * gain).astype(BF)

    low_rows = query_weight.shape[0]
    attn_columns = [
        w.reshape(low_rows, 2, 2, part)
        for w in (
            scaled(query_weight, gain_attn),
            scaled(key_weight, gain_attn),
            scaled(value_weight, gain_attn),
            output_weight.T,
        )
    ]
    attn_pieces = jnp.stack(
        [jnp.concatenate(attn_columns[i : i + 2], axis=3) for i in (0, 2)], axis=1
    )
    attn_pieces = attn_pieces.reshape(low_rows, 2, 2, 4 * part).transpose(2, 1, 0, 3)
    own_in = layer_input.astype(F32)
    own = rms_unit(own_in)[0].astype(BF)

    attn_cores, own, other, gain = stage(
        exchange_cores(attn_pieces), own, swap(own, "c"), gain_mlp
    )

    attn_block = exchange_chips(attn_cores).reshape(-1, 4 * part)
    attn_block, own, other = stage(attn_block, own, other)

    attn_line, p_mine = gather_line(attn_block), hop(own)
    mlp_weights = [scaled(gate_weight, gain), scaled(up_weight, gain), down_weight.T]
    mlp_cores = exchange_cores(to_pieces(mlp_weights, [wide] * 3))
    attn_line, p_mine, s_other, other, (spot, even_tables, odd_tables) = stage(
        attn_line, p_mine, swap(p_mine, "c"), other, places(half)
    )

    near_lines, p_other = gather_plane(attn_line), hop(other)
    mlp_block = exchange_chips(after(mlp_cores, p_mine)).reshape(-1, 3 * wide)
    swapped = [swap(attn_line, "c")]
    near_lines, p_other, mlp_block, p_mine, swapped = stage(
        near_lines, p_other, mlp_block, p_mine, swapped
    )

    mlp_weight = lax.all_gather(mlp_block, ("y", "x"), axis=0, tiled=True)
    far_lines, far = gather_far_line(*near_lines), hop(p_mine)
    swapped += [swap(v, "c") for v in near_lines]
    odd_in = (p_mine, swap(p_other, "c"), p_other, s_other)
    far_lines, far = stage(far_lines, far)

    grad_mine, other_grad = hop(after(out_grad, p_other)), swap(out_grad, "c")
    grad_other = hop(after(other_grad, far))
    near_grad = (out_grad, other_grad)
    odd_grad = (grad_mine, swap(grad_other, "c"), grad_other, swap(grad_mine, "c"))

    lines = (attn_line, *near_lines, *far_lines, *swapped, *(swap(v, "c") for v in far_lines))
    odd_at = attend(ODD, spot, odd_in, lines, odd_tables)
    attn_weight = odd_at[4]
    even_in = after((own, far, other, swap(far, "c")), attn_weight)
    even_at = attend(EVEN, spot, even_in, attn_weight, even_tables)
    even_sums = after(even_at[2:4], grad_mine, grad_other)
    hidden = own_in + total(relayed_sum(even_sums, odd_at[2:4]))

    near_mid, odd_mid = gather_odd(rms_unit(hidden)[0].astype(BF))
    odd_feed = feed(ODD, odd_mid, odd_grad, mlp_weight, units)
    even_mid = gather_far(near_mid, odd_mid, odd_feed[0])
    even_grad = gather_far(near_grad, odd_grad, odd_feed[0])
    even_feed = feed(EVEN, even_mid, even_grad, mlp_weight, units)
    mlp_partial = feed_weights(
        even_mid + odd_mid,
        even_grad + odd_grad,
        (even_feed[1], odd_feed[1]),
        (even_feed[0], odd_feed[0]),
        3,
    )
    terms = direct_sum(even_feed[4:], odd_feed[4:], (even_mid[1], even_grad[1]), mlp_partial)
    mlp_sum = lax.psum_scatter(
        after(mlp_partial, terms[-2]), ("y", "x"), scatter_dimension=0, tiled=True
    )
    grad_hidden = norm_back(terms, hidden, out_grad)

    near_hidden, odd_hidden = gather_odd(grad_hidden)
    odd_back = attend_back(ODD, spot, odd_hidden, odd_at[0], attn_weight, odd_tables)
    even_hidden = gather_far(near_hidden, odd_hidden, odd_back[0])
    even_back = attend_back(EVEN, spot, even_hidden, even_at[0], attn_weight, even_tables)
    got, side = swap(even_back[2], "c"), swap(odd_back[2], "c")
    keep, send = attend_weights(
        spot,
        even_in + odd_in,
        even_hidden + odd_hidden,
        (even_back[0], odd_back[0]),
        (even_at[1], odd_at[1]),
    )
    keep, send, got, side = stage(keep, send, got, side)

    def both(i):
        return jnp.concatenate([keep[i], swap(send[i], "c")], axis=-1)

    def finish(odd, side, relayed):
        last = hop(jnp.concatenate(near_sums(odd, side, relayed)))
        return last, swap(last, "c")

    relayed1, relayed3 = reduce_far(both(2))
    relayed = hop(far_sum(even_back[1:], got))
    out_even, out_odd = after((even_feed[2:4], odd_feed[2:4]), got)
    out_got, out_side = swap(out_even[1], "c"), swap(out_odd[1], "c")
    parts = both(0), both(1), both(3)
    relayed1, relayed3, relayed, parts, out_got, out_side = stage(
        relayed1, relayed3, relayed, parts, out_got, out_side
    )

    attn_line = reduce_near(parts[0], *near_operands(*parts[1:], relayed1, relayed3))
    last, crossed = finish(odd_back[1:], side, relayed)
    out_relayed = hop(far_sum(out_even, out_got))
    mlp_cores = exchange_cores(mlp_sum.reshape(2, 2, -1, mlp_sum.shape[1]))
    attn_line, last, crossed = stage(attn_line, last, crossed)

    attn_sum, mlp_own = reduce_line(attn_line), exchange_chips(mlp_cores)
    out_last, out_crossed = finish(out_odd, out_side, out_relayed)
    input_grad = norm_back((even_back[1], got, last, crossed), layer_input, grad_hidden)
    attn_sum, mlp_own, input_grad = stage(attn_sum, mlp_own, input_grad)
    layer_output = (hidden + total((out_even[0], out_got, out_last[:half], out_crossed))).astype(BF)

    def whole(pieces, start, size):
        piece = pieces[..., start : start + size].reshape(4, -1, size)
        return piece.transpose(1, 0, 2).reshape(-1, 4 * size).astype(F32)

    def gain_of(pairs):
        return sum(jnp.sum(w.astype(F32) * g, axis=1) for w, g in pairs)

    size = 2 * part
    core = lax.axis_index("c")
    attn_sum = jnp.where(core == 0, attn_sum, jnp.roll(attn_sum, size, axis=1)).astype(BF)
    attn_cores = exchange_cores(attn_sum.reshape(2, 2, -1, 2 * size))
    starts = (0, units, together(units))
    gate_own, up_own, down_own = (whole(mlp_own, start, units) for start in starts)
    gate_grad, up_grad = gate_own * gain_mlp, up_own * gain_mlp
    mlp_gain = gain_of([(gate_weight, gate_own), (up_weight, up_own)])
    attn_cores, gate_grad, up_grad, down_own, mlp_gain = stage(
        attn_cores, gate_grad, up_grad, down_own, mlp_gain
    )
    attn_own = exchange_chips(attn_cores)

    def attn_whole(kind, start):
        piece = attn_own[:, kind].reshape(2, low_rows, 2, size)[..., start : start + part]
        return piece.transpose(1, 0, 2, 3).reshape(low_rows, 4 * part).astype(F32)

    query_own, key_own, value_own, output_own = (
        attn_whole(kind, start) for kind in (0, 1) for start in (0, part)
    )
    gains = jnp.stack(
        [
            gain_of([(query_weight, query_own), (key_weight, key_own), (value_weight, value_own)]),
            mlp_gain,
        ]
    )
    attn_gain, mlp_gain = gains + swap(gains, "t")
    return (
        layer_output,
        input_grad,
        attn_gain,
        query_own * gain_attn,
        key_own * gain_attn,
        value_own * gain_attn,
        output_own.T,
        mlp_gain,
        gate_grad,
        up_grad,
        down_own.T,
    )


def solution(mesh):
    devices = mesh.devices.reshape(4, 4, 2, 2, 2)
    fine = Mesh(devices, ("y", "x", "l", "c", "t"))
    rows = P(GROUP + ("t",), None)
    gain, into, out = P(GROUP), P(GROUP, "t"), P("t", GROUP)
    return jax.shard_map(
        shards,
        mesh=fine,
        in_specs=(rows, gain, into, into, into, out, gain, into, into, out, rows),
        out_specs=(rows, rows, gain, into, into, into, out, gain, into, into, out),
        check_vma=False,
    )
```

```python
import functools
import math

import jax
import jax.numpy as jnp
from jax import lax
from jax.experimental import pallas as pl
from jax.experimental.pallas import tpu as pltpu
from jax.sharding import Mesh, PartitionSpec as P

HD = 128
EPSILON = 1e-05
ROPE_BASE = 10000.0
MASKED = -1e30
BF = jnp.bfloat16
F32 = jnp.float32

GROUP = ("y", "x", "l", "c")
RING = ("l", "c", "t")


def plain(left, right):
    return jnp.dot(left, right, preferred_element_type=F32)


def times_t(left, right):
    return lax.dot_general(left, right, (((1,), (1,)), ((), ())), preferred_element_type=F32)


def left_t(left, right):
    return lax.dot_general(left, right, (((0,), (0,)), ((), ())), preferred_element_type=F32)


def swap(values, axis):
    return lax.ppermute(values, axis, [(0, 1), (1, 0)])


def hop(values):
    def place(z, core):
        return (z % 2) * 4 + core * 2 + z // 2

    pairs = []
    for z in range(4):
        pairs.append((place(z, 0), place((z + 1) % 4, 0)))
        pairs.append((place(z, 1), place((z + 3) % 4, 1)))
    return lax.ppermute(values, RING, pairs)


def after(values, *others):
    return lax.optimization_barrier((values, *others))[0]


def stage(*values):
    return lax.optimization_barrier(values)


EVEN, ODD = "even", "odd"


def gather_odd(rows):
    other = swap(rows, "c")
    p_mine, p_other = hop(rows), hop(other)
    return (rows, other), (p_mine, swap(p_other, "c"), p_other, swap(p_mine, "c"))


def gather_far(near, odd, *others):
    far = hop(after(odd[0], odd[1], odd[3]))
    return (near[0], far, near[1], swap(after(far, *others), "c"))


def far_sum(even, got):
    rows = got.shape[0] // 2
    return (even[0][rows:].astype(F32) + got[rows:].astype(F32)).astype(BF)


def near_sums(odd, side, relayed):
    rows = relayed.shape[0]
    mine = odd[0][:rows].astype(F32) + side[:rows].astype(F32) + relayed.astype(F32)
    other = odd[0][rows:].astype(F32) + side[rows:].astype(F32)
    return mine.astype(BF), other.astype(BF)


def fold(even, got):
    rows = got.shape[0] // 2
    own = even[0][:rows].astype(F32) + got[:rows].astype(F32)
    return stage(far_sum(even, got), own)


def relayed_sum(even, odd):
    rows = even[0].shape[0] // 2
    side = swap(odd[1], "c")
    other = hop((odd[0][rows:].astype(F32) + side[rows:].astype(F32)).astype(BF))
    far, own = fold(even, swap(even[1], "c"))
    relayed = hop(far)
    mine = odd[0][:rows].astype(F32) + side[:rows].astype(F32) + relayed.astype(F32)
    return own, hop(mine.astype(BF)), swap(other, "c")


def direct_sum(even, odd, side_after, *others):
    side = swap(after(odd[1], *side_after), "c")
    pair = hop((odd[0].astype(F32) + side.astype(F32)).astype(BF))
    got = swap(even[1], "c")
    terms = swap(far_sum(even, got), "t"), pair, swap(pair, "c")
    far, pair, crossed = after(terms, *others)
    return even[0], got, pair, far, crossed


def total(terms):
    rows = terms[-2].shape[0]
    last = terms[-1][-rows:]
    return sum(term[:rows].astype(F32) for term in terms[:-1]) + last.astype(F32)


VMEM = pl.BlockSpec(memory_space=pltpu.VMEM)
SMEM = pl.BlockSpec(memory_space=pltpu.SMEM)


def exchange_cores(pieces):
    core = lax.axis_index("c")
    mine = jnp.where(core == 0, pieces[:, 0], pieces[:, 1])
    theirs = swap(jnp.where(core == 0, pieces[:, 1], pieces[:, 0]), "c")
    return jnp.stack(
        [jnp.where(core == 0, mine, theirs), jnp.where(core == 0, theirs, mine)], axis=1
    )


def exchange_chips(cores):
    low = lax.axis_index("l")
    mine = jnp.where(low == 0, cores[0], cores[1])
    theirs = swap(jnp.where(low == 0, cores[1], cores[0]), "l")
    return jnp.stack([jnp.where(low == 0, mine, theirs), jnp.where(low == 0, theirs, mine)], axis=0)


def split_pieces(weight, width):
    rows, columns = weight.shape
    pieces = weight.reshape(rows, 4, columns // 4)
    return jnp.pad(pieces, ((0, 0), (0, 0), (0, width - columns // 4)))


def to_pieces(weights, widths):
    joined = jnp.concatenate([split_pieces(w, n) for w, n in zip(weights, widths)], axis=2)
    rows = joined.shape[0]
    return joined.transpose(1, 0, 2).reshape(2, 2, rows, joined.shape[2])


PLANE = ("y", "x", "c")


def along(values, distance, second):
    pairs = []
    for place in range(32):
        y, x, core = place // 8, place // 2 % 4, place % 2
        if (core == 0) != second:
            target = (y, (x + distance) % 4, core)
        else:
            target = ((y + distance) % 4, x, core)
        pairs.append((place, (target[0] * 4 + target[1]) * 2 + target[2]))
    return lax.ppermute(values, PLANE, pairs)


def gather_line(block):
    return jnp.stack([block] + [along(block, -d, False) for d in (1, 2, 3)])


def gather_plane(line):
    return along(line, -1, True), along(line, 1, True)


def gather_far_line(after1, after3):
    half = after1.shape[0] // 2
    return along(after1[:half], -1, True), along(after3[half:], 1, True)


def reduce_far(part):
    return along(part[:2], 1, False), along(part[2:], -1, False)


def near_operands(part1, part3, relayed1, relayed3):
    to1 = (part1[:2].astype(F32) + relayed1.astype(F32)).astype(BF)
    to3 = (part3[2:].astype(F32) + relayed3.astype(F32)).astype(BF)
    return jnp.concatenate([to1, part1[2:]]), jnp.concatenate([part3[:2], to3])


def reduce_near(part0, to1, to3):
    from1, from3 = along(to1, 1, False), along(to3, -1, False)
    return (part0.astype(F32) + from1.astype(F32) + from3.astype(F32)).astype(BF)


def reduce_line(line):
    total = line[0].astype(F32)
    for d in (1, 3, 2):
        total = total + along(line[d], d, True).astype(F32)
    return total


def rms_unit(rows):
    inv = lax.rsqrt(jnp.mean(rows * rows, axis=-1, keepdims=True) + EPSILON)
    return rows * inv, inv


def rms_back(grad_unit, unit, inv):
    return inv * (grad_unit - unit * jnp.mean(grad_unit * unit, axis=-1, keepdims=True))


def places(half):
    core = lax.axis_index("c")
    ring = lax.axis_index("t") * 2 + lax.axis_index("l")
    start = jnp.stack([ring // 2, ((ring + 3 - 2 * core) % 4) // 2]).astype(jnp.int32) * half
    length = 2 * half
    frequency = ROPE_BASE ** (-jnp.arange(HD // 2, dtype=F32) * 2.0 / HD)
    angles = jnp.arange(length, dtype=F32)[:, None] * frequency[None, :]
    cosine, sine = jnp.cos(angles), jnp.sin(angles)
    tables = []
    for i in range(2):
        for table in (jnp.concatenate([cosine] * 2, 1), jnp.concatenate([-sine, sine], 1)):
            tables.append(jnp.where(start[i] == 0, table, jnp.roll(table, half, axis=0)))
    spot = jnp.concatenate([start, jnp.stack([lax.axis_index(a) for a in ("c", "y", "x")])])
    return spot.astype(jnp.int32), tables[:2], tables[2:]


HBM = pl.BlockSpec(memory_space=pltpu.HBM)


LIMIT = pltpu.CompilerParams(vmem_limit_bytes=32 * 2**20)


def cost(us):
    return pl.CostEstimate(flops=int(us * 1.1e9), bytes_accessed=0, transcendentals=0)


def kernel_call(body, shapes, us, args, specs, scratch, name):
    return pl.pallas_call(
        body,
        out_shape=[jax.ShapeDtypeStruct(shape, BF) for shape in shapes],
        in_specs=specs,
        out_specs=[VMEM] * len(shapes),
        scratch_shapes=list(scratch),
        compiler_params=LIMIT,
        cost_estimate=cost(us),
        name=name,
    )(*args)


def wait_all(copies):
    for copy in copies:
        copy.wait()


def causal_mask(start, length):
    def place(dim):
        index = lax.broadcasted_iota(jnp.int32, (length, length), dim) + start
        return jnp.where(index >= length, index - length, index)

    return place(0) >= place(1)


def soft_weights(query, key, mask):
    scores = jnp.where(mask, times_t(query, key) * (1.0 / math.sqrt(HD)), MASKED)
    weights = jnp.exp(scores - jnp.max(scores, axis=-1, keepdims=True))
    return weights / jnp.sum(weights, axis=-1, keepdims=True)


def turned(values, cosine, sine):
    return values * cosine + pltpu.roll(values, HD // 2, 1) * sine


def fetch(pairs, sems, first=0):
    copies = [pltpu.make_async_copy(a, b, sems.at[first + i]) for i, (a, b) in enumerate(pairs)]
    for copy in copies:
        copy.start()
    return copies


def joined(blocks, target, first=0):
    rows = blocks[0].shape[0]
    return [
        (block, target.at[pl.ds(first + rows * n, rows), :]) for n, block in enumerate(blocks)
    ]


def feature_block(core, y, x, first, second):
    dy, dx = jnp.where(core == 0, second, first), jnp.where(core == 0, first, second)
    return lax.rem(y + dy, 4) * 4 + lax.rem(x + dx, 4)


def plane_blocks(spot, lines, target):
    core, y, x = spot[2], spot[3], spot[4]
    rows, size = lines[0].shape[1], lines[0].shape[2] // 2
    half = pl.ds(pl.multiple_of(core * size, size), size)
    pairs = []
    for kind, group in ((core, lines[:5]), (1 - core, lines[5:])):
        columns = pl.ds(pl.multiple_of(kind * size, size), size)
        for second in range(4):
            for first in range(4):
                row = pl.multiple_of(feature_block(kind, y, x, first, second) * rows, rows)
                if second == 2:
                    source = group[3 + first // 2].at[first % 2, :, half]
                else:
                    source = group[(0, 1, None, 2)[second]].at[first, :, half]
                pairs.append((source, target.at[pl.ds(row, rows), columns]))
    return pairs


OUTS = {EVEN: ((0, 0), (0, 1), (1, 0), (1, 1)), ODD: ((1, 1), (0, 0), (1, 0), (0, 1))}


def product_t(left, weight, targets, slots, chunk):
    rows = left.shape[0] // 4

    def step(i, carry):
        part = pl.ds(pl.multiple_of(i * chunk, chunk), chunk)
        found = times_t(left[...], weight[part, :]).astype(BF)
        for n, (target, block) in enumerate(OUTS[slots]):
            place = slice(rows * block, rows * (block + 1))
            targets[target][place, part] = found[rows * n : rows * (n + 1)]
        return carry

    lax.fori_loop(0, weight.shape[0] // chunk, step, 0)


def norm_back_kernel(count, *refs):
    staged, sems = refs[count + 3 : -1], refs[-1]
    rows = staged[0].shape[0]
    starts = [0] * count + [0, 0]
    starts[count - 1] = refs[count - 1].shape[0] - rows
    pairs = [(ref.at[pl.ds(first, rows), :], to) for ref, first, to in zip(refs, starts, staged)]
    wait_all(fetch(pairs, sems))
    grad = sum(ref[...].astype(F32) for ref in staged[:count])
    unit, inv = rms_unit(staged[count][...].astype(F32))
    base = staged[count + 1][...].astype(F32)
    refs[count + 2][...] = (base + rms_back(grad, unit, inv)).astype(BF)


def norm_back(terms, rows, base):
    args = (*terms, rows, base)
    return pl.pallas_call(
        functools.partial(norm_back_kernel, len(terms)),
        out_shape=jax.ShapeDtypeStruct(rows.shape, BF),
        in_specs=[HBM] * len(args),
        out_specs=VMEM,
        scratch_shapes=[pltpu.VMEM(rows.shape, a.dtype) for a in args]
        + [pltpu.SemaphoreType.DMA((len(args),))],
        compiler_params=pltpu.CompilerParams(vmem_limit_bytes=60 * 2**20),
        cost_estimate=cost(0),
        name="norm_back",
    )(*args)


def attend_kernel(slots, spot, *refs):
    if slots is ODD:
        n = len(refs) - 9
        arrays, lines, (cosine, sine) = refs[:4], refs[4:n], refs[n : n + 2]
        qkv, heads_cat, kept, sent, weight, rows, sems = refs[n + 2 :]
        copies = plane_blocks(spot, lines, weight)
    else:
        arrays, (weight, cosine, sine) = refs[:4], refs[4:7]
        qkv, heads_cat, kept, sent, rows, sems = refs[7:]
        copies = []
    part = weight.shape[1] // 4
    length = cosine.shape[0]
    wait_all(fetch(joined(arrays, rows) + copies, sems))
    both = plain(rows[...], weight[:, : 3 * part])
    qkv[:, 2 * part :] = both[:, 2 * part :].astype(BF)
    mask = causal_mask(spot[0 if slots is EVEN else 1], length)
    for s in range(2):
        here = slice(s * length, (s + 1) * length)
        for i in range(part // HD):
            columns = slice(i * HD, (i + 1) * HD)
            others = slice(part + i * HD, part + (i + 1) * HD)
            values = slice(2 * part + i * HD, 2 * part + (i + 1) * HD)
            query = turned(both[here, columns], cosine[...], sine[...]).astype(BF)
            key = turned(both[here, others], cosine[...], sine[...]).astype(BF)
            qkv[here, columns] = query
            qkv[here, others] = key
            soft = soft_weights(query, key, mask).astype(BF)
            heads_cat[here, columns] = plain(soft, qkv[here, values]).astype(BF)
    product_t(heads_cat, weight.at[:, 3 * part :], (kept, sent), slots, 512)


def size_of(arrays):
    return sum(array.shape[0] for array in arrays), arrays[0].shape[1]


def attend(slots, spot, arrays, weights, tables):
    rows, width = size_of(arrays)
    odd = slots is ODD
    part = (weights[0] if odd else weights).shape[-1] // 4
    weights = list(weights) if odd else [weights]
    return kernel_call(
        functools.partial(attend_kernel, slots),
        [(rows, 3 * part), (rows, part), (rows // 2, width), (rows // 2, width)]
        + [(width, 4 * part)] * odd,
        0 if odd else 2,
        (spot, *arrays, *weights, *tables),
        [SMEM] + [HBM] * len(arrays) + [HBM if odd else VMEM] * len(weights) + [VMEM] * 2,
        [pltpu.VMEM((rows, width), BF), pltpu.SemaphoreType.DMA((36,))],
        name="attend",
    )


def attend_back_kernel(slots, spot, *refs):
    arrays, (weight, qkv_in, cosine, sine) = refs[:4], refs[4:8]
    grad_qkv, kept, sent, rows, qkv, sems = refs[8:]
    part = weight.shape[1] // 4
    length = cosine.shape[0]
    factor = 1.0 / math.sqrt(HD)
    wait_all(fetch(joined(arrays, rows) + [(qkv_in, qkv)], sems))
    grad_heads = plain(rows[...], weight[:, 3 * part :]).astype(BF)
    mask = causal_mask(spot[0 if slots is EVEN else 1], length)
    for s in range(2):
        here = slice(s * length, (s + 1) * length)
        for i in range(part // HD):
            columns = slice(i * HD, (i + 1) * HD)
            others = slice(part + i * HD, part + (i + 1) * HD)
            values = slice(2 * part + i * HD, 2 * part + (i + 1) * HD)
            query, key = qkv[here, columns], qkv[here, others]
            soft = soft_weights(query, key, mask)
            grad_mix = grad_heads[here, columns]
            grad_soft = times_t(grad_mix, qkv[here, values])
            grad_qkv[here, values] = left_t(soft.astype(BF), grad_mix).astype(BF)
            inner = jnp.sum(grad_soft * soft, axis=-1, keepdims=True)
            grad_scores = (soft * (grad_soft - inner)).astype(BF)
            back_q = plain(grad_scores, key) * factor
            back_k = left_t(grad_scores, query) * factor
            grad_qkv[here, columns] = turned(back_q, cosine[...], -sine[...]).astype(BF)
            grad_qkv[here, others] = turned(back_k, cosine[...], -sine[...]).astype(BF)
    product_t(grad_qkv, weight.at[:, : 3 * part], (kept, sent), slots, 512)


def attend_back(slots, spot, arrays, qkv, weight, tables):
    rows, width = size_of(arrays)
    part = weight.shape[1] // 4
    return kernel_call(
        functools.partial(attend_back_kernel, slots),
        [(rows, 3 * part), (rows // 2, width), (rows // 2, width)],
        0,
        (spot, *arrays, weight, qkv, *tables),
        [SMEM] + [HBM] * 4 + [VMEM, HBM] + [VMEM] * 2,
        [pltpu.VMEM((rows, width), BF), pltpu.VMEM((rows, 3 * part), BF)]
        + [pltpu.SemaphoreType.DMA((5,))],
        name="attend_back",
    )


def sent_product_t(left, weight, staged, targets, slots, sems, first):
    rows, chunk = left.shape[0] // 4, weight.shape[0] // 4
    copies = []
    for i in range(4):
        part = pl.ds(i * chunk, chunk)
        staged[:, part] = times_t(left[...], weight[part, :]).astype(BF)
        pairs = [
            (
                staged.at[pl.ds(rows * n, rows), part],
                targets[target].at[pl.ds(rows * block, rows), part],
            )
            for n, (target, block) in enumerate(OUTS[slots])
        ]
        copies += fetch(pairs, sems, first + 4 * i)
    return copies


def feed_kernel(slots, units, *refs):
    arrays, gradients, source = refs[:4], refs[4:8], refs[8]
    activation_out, grad_gu_out, kept, sent, grad_kept, grad_sent = refs[9:15]
    activation, grad_gu, compact, staged, grad_staged, rows, grads, weight, sems = refs[15:]
    wide = weight.shape[1] // 3
    chunk = min(256, wide)
    chunks = wide // chunk
    row_copies = fetch(joined(arrays, rows), sems)

    def part(kind, i):
        return pl.ds(wide * kind + chunk * i, chunk)

    def load(kind, i):
        columns = part(kind, i)
        return fetch([(source.at[:, columns], weight.at[:, columns])], sems, 8 + 3 * i + kind)

    gate_up_copies = [load(0, i) + load(1, i) for i in range(chunks)]
    grad_copies = fetch(joined(gradients, grads), sems, 4)
    down_copies = [load(2, i) for i in range(chunks)]
    wait_all(row_copies)
    found = []
    for i in range(chunks):
        wait_all(gate_up_copies[i])
        found.append([plain(rows[...], weight[:, part(kind, i)]) for kind in range(2)])
    wait_all(grad_copies)
    for copies in down_copies:
        wait_all(copies)
    for i in range(chunks):
        gate, up = found[i]
        grad_act = plain(grads[...], weight[:, part(2, i)])
        sigmoid = jax.nn.sigmoid(gate)
        swish = gate * sigmoid
        activation[:, part(0, i)] = (swish * up).astype(BF)
        grad_gate = grad_act * up * (sigmoid + swish * (1.0 - sigmoid))
        grad_gu[:, part(0, i)] = grad_gate.astype(BF)
        grad_gu[:, part(1, i)] = (grad_act * swish).astype(BF)
    compact[:, :units] = grad_gu[:, :units]
    compact[:, units : 2 * units] = grad_gu[:, wide : wide + units]
    compact[:, 2 * units :] = jnp.zeros_like(compact[:, 2 * units :])
    copies = fetch([(activation, activation_out), (compact, grad_gu_out)], sems)
    down, gate_up = weight.at[:, 2 * wide :], weight.at[:, : 2 * wide]
    copies += sent_product_t(activation, down, staged, (kept, sent), slots, sems, 2)
    copies += sent_product_t(
        grad_gu, gate_up, grad_staged, (grad_kept, grad_sent), slots, sems, 18
    )
    wait_all(copies)


def together(units):
    return -(-2 * units // 128) * 128


def feed(slots, arrays, grads, weight, units):
    rows, width = size_of(arrays)
    wide = weight.shape[1] // 3
    shapes = [(rows, wide), (rows, together(units))]
    scratch = [(rows, wide), (rows, 2 * wide), shapes[1]]
    scratch += [(rows, width)] * 4 + [(width, 3 * wide)]
    shapes += [(rows // 2, width)] * 4
    return pl.pallas_call(
        functools.partial(feed_kernel, slots, units),
        out_shape=[jax.ShapeDtypeStruct(shape, BF) for shape in shapes],
        in_specs=[HBM] * (2 * len(arrays) + 1),
        out_specs=[HBM] * len(shapes),
        scratch_shapes=[pltpu.VMEM(shape, BF) for shape in scratch]
        + [pltpu.SemaphoreType.DMA((34,))],
        compiler_params=pltpu.CompilerParams(vmem_limit_bytes=60 * 2**20),
        cost_estimate=cost(0 if slots is ODD else 8),
        name="feed",
    )(*arrays, *grads, weight)


def feed_weights_kernel(start, *refs):
    grad_gus, activations, out = refs[16:18], refs[18:20], refs[20]
    rows, grads, grad_gu, activation, staged, sems = refs[21:]
    middle = grad_gu.shape[0] // 2

    def pair(halves, target):
        return [(half, target.at[pl.ds(middle * i, middle), :]) for i, half in enumerate(halves)]

    first = fetch(joined(refs[:8], rows) + pair(grad_gus, grad_gu), sems)
    second = fetch(joined(refs[8:16], grads) + pair(activations, activation), sems, 10)
    wait_all(first)
    tile = 256
    outs = []
    for i in range(rows.shape[1] // tile):
        part = pl.ds(tile * i, tile)
        staged[part, :start] = left_t(rows[:, part], grad_gu[...]).astype(BF)
        if i == 0:
            wait_all(second)
        staged[part, start:] = left_t(grads[:, part], activation[...]).astype(BF)
        outs += fetch([(staged.at[part, :], out.at[part, :])], sems, 20 + i)
    wait_all(outs)


def feed_weights(rows, grads, grad_gus, activations, us):
    count, width = rows[0].shape
    sizes = [grad_gus[0].shape[1], activations[0].shape[1]]
    args = (*rows, *grads, *grad_gus, *activations)
    shapes = [(8 * count, width)] * 2 + [(8 * count, n) for n in sizes] + [(width, sum(sizes))]
    return pl.pallas_call(
        functools.partial(feed_weights_kernel, sizes[0]),
        out_shape=jax.ShapeDtypeStruct((width, sum(sizes)), BF),
        in_specs=[HBM] * len(args),
        out_specs=HBM,
        scratch_shapes=[pltpu.VMEM(shape, BF) for shape in shapes]
        + [pltpu.SemaphoreType.DMA((20 + width // 256,))],
        compiler_params=pltpu.CompilerParams(vmem_limit_bytes=60 * 2**20),
        cost_estimate=cost(us),
        name="feed_weights",
    )(*args)


def attend_weights_kernel(spot, *refs):
    grads, heads = refs[16:18], refs[18:20]
    keeps, sends, (ins, hiddens, sems) = refs[20:24], refs[24:28], refs[28:]
    wait_all(fetch(joined(refs[:8], ins) + joined(refs[8:16], hiddens), sems))
    tile, size = keeps[0].shape[1:]

    def step(first, j):
        columns = []
        for second in (j, j + 1):
            block = feature_block(spot[2], spot[3], spot[4], first, second)
            columns.append(pl.ds(pl.multiple_of(block * tile, tile), tile))
        found = []
        for rows, rights in ((ins, grads), (hiddens, heads)):
            left = jnp.concatenate([rows[:, c] for c in columns], axis=1)
            right = jnp.concatenate([r[...] for r in rights], axis=0)
            found.append(left_t(left, right).astype(BF))
        both = jnp.concatenate(found, axis=1)
        left, right = both[:, :size], both[:, size:]
        kept = jnp.where(spot[2] == 0, left, right)
        sent = jnp.where(spot[2] == 0, right, left)
        for k in range(2):
            keeps[first][j + k] = kept[tile * k : tile * (k + 1)]
            sends[j + k][first] = sent[tile * k : tile * (k + 1)]

    for first in range(4):
        for j in (0, 2):
            step(first, j)


def attend_weights(spot, ins, hiddens, grads, heads):
    rows, width = ins[0].shape
    tile = width // 16
    size = (grads[0].shape[1] + heads[0].shape[1]) // 2
    found = kernel_call(
        attend_weights_kernel,
        [(4, tile, size)] * 8,
        0,
        (spot, *ins, *hiddens, *grads, *heads),
        [SMEM] + [HBM] * 16 + [VMEM] * 4,
        [pltpu.VMEM((8 * rows, width), BF)] * 2 + [pltpu.SemaphoreType.DMA((16,))],
        name="attend_weights",
    )
    return found[:4], found[4:]


def shards(
    layer_input,
    attn_scale,
    query_weight,
    key_weight,
    value_weight,
    output_weight,
    mlp_scale,
    gate_weight,
    up_weight,
    down_weight,
    out_grad,
):
    half, width = layer_input.shape
    gain_attn = attn_scale.astype(F32)[:, None]
    gain_mlp = mlp_scale.astype(F32)[:, None]
    part = query_weight.shape[1] // 4
    units = gate_weight.shape[1] // 4
    wide = -(-units // 128) * 128

    def scaled(weight, gain):
        return (weight.astype(F32) * gain).astype(BF)

    low_rows = query_weight.shape[0]
    attn_columns = [
        w.reshape(low_rows, 2, 2, part)
        for w in (
            scaled(query_weight, gain_attn),
            scaled(key_weight, gain_attn),
            scaled(value_weight, gain_attn),
            output_weight.T,
        )
    ]
    attn_pieces = jnp.stack(
        [jnp.concatenate(attn_columns[i : i + 2], axis=3) for i in (0, 2)], axis=1
    )
    attn_pieces = attn_pieces.reshape(low_rows, 2, 2, 4 * part).transpose(2, 1, 0, 3)
    own_in = layer_input.astype(F32)
    own = rms_unit(own_in)[0].astype(BF)

    attn_cores, own, other, gain = stage(
        exchange_cores(attn_pieces), own, swap(own, "c"), gain_mlp
    )

    attn_block = exchange_chips(attn_cores).reshape(-1, 4 * part)
    attn_block, own, other = stage(attn_block, own, other)

    attn_line, p_mine = gather_line(attn_block), hop(own)
    mlp_weights = [scaled(gate_weight, gain), scaled(up_weight, gain), down_weight.T]
    mlp_cores = exchange_cores(to_pieces(mlp_weights, [wide] * 3))
    attn_line, p_mine, s_other, other, (spot, even_tables, odd_tables) = stage(
        attn_line, p_mine, swap(p_mine, "c"), other, places(half)
    )

    near_lines, p_other = gather_plane(attn_line), hop(other)
    mlp_block = exchange_chips(after(mlp_cores, p_mine)).reshape(-1, 3 * wide)
    swapped = [swap(attn_line, "c")]
    near_lines, p_other, mlp_block, p_mine, swapped = stage(
        near_lines, p_other, mlp_block, p_mine, swapped
    )

    mlp_weight = lax.all_gather(mlp_block, ("y", "x"), axis=0, tiled=True)
    far_lines, far = gather_far_line(*near_lines), hop(p_mine)
    swapped += [swap(v, "c") for v in near_lines]
    odd_in = (p_mine, swap(p_other, "c"), p_other, s_other)
    far_lines, far = stage(far_lines, far)

    grad_mine, other_grad = hop(after(out_grad, p_other)), swap(out_grad, "c")
    grad_other = hop(after(other_grad, far))
    near_grad = (out_grad, other_grad)
    odd_grad = (grad_mine, swap(grad_other, "c"), grad_other, swap(grad_mine, "c"))

    lines = (attn_line, *near_lines, *far_lines, *swapped, *(swap(v, "c") for v in far_lines))
    odd_at = attend(ODD, spot, odd_in, lines, odd_tables)
    attn_weight = odd_at[4]
    even_in = after((own, far, other, swap(far, "c")), attn_weight)
    even_at = attend(EVEN, spot, even_in, attn_weight, even_tables)
    even_sums = after(even_at[2:4], grad_mine, grad_other)
    hidden = own_in + total(relayed_sum(even_sums, odd_at[2:4]))

    near_mid, odd_mid = gather_odd(rms_unit(hidden)[0].astype(BF))
    odd_feed = feed(ODD, odd_mid, odd_grad, mlp_weight, units)
    even_mid = gather_far(near_mid, odd_mid, odd_feed[0])
    even_grad = gather_far(near_grad, odd_grad, odd_feed[0])
    even_feed = feed(EVEN, even_mid, even_grad, mlp_weight, units)
    mlp_partial = feed_weights(
        even_mid + odd_mid,
        even_grad + odd_grad,
        (even_feed[1], odd_feed[1]),
        (even_feed[0], odd_feed[0]),
        3,
    )
    terms = direct_sum(even_feed[4:], odd_feed[4:], (even_mid[1], even_grad[1]), mlp_partial)
    mlp_sum = lax.psum_scatter(
        after(mlp_partial, terms[-2]), ("y", "x"), scatter_dimension=0, tiled=True
    )
    grad_hidden = norm_back(terms, hidden, out_grad)

    near_hidden, odd_hidden = gather_odd(grad_hidden)
    odd_back = attend_back(ODD, spot, odd_hidden, odd_at[0], attn_weight, odd_tables)
    even_hidden = gather_far(near_hidden, odd_hidden, odd_back[0])
    even_back = attend_back(EVEN, spot, even_hidden, even_at[0], attn_weight, even_tables)
    got, side = swap(even_back[2], "c"), swap(odd_back[2], "c")
    keep, send = attend_weights(
        spot,
        even_in + odd_in,
        even_hidden + odd_hidden,
        (even_back[0], odd_back[0]),
        (even_at[1], odd_at[1]),
    )
    keep, send, got, side = stage(keep, send, got, side)

    def both(i):
        return jnp.concatenate([keep[i], swap(send[i], "c")], axis=-1)

    def finish(odd, side, relayed):
        last = hop(jnp.concatenate(near_sums(odd, side, relayed)))
        return last, swap(last, "c")

    relayed1, relayed3 = reduce_far(both(2))
    relayed = hop(far_sum(even_back[1:], got))
    out_even, out_odd = after((even_feed[2:4], odd_feed[2:4]), got)
    out_got, out_side = swap(out_even[1], "c"), swap(out_odd[1], "c")
    parts = both(0), both(1), both(3)
    relayed1, relayed3, relayed, parts, out_got, out_side = stage(
        relayed1, relayed3, relayed, parts, out_got, out_side
    )

    attn_line = reduce_near(parts[0], *near_operands(*parts[1:], relayed1, relayed3))
    last, crossed = finish(odd_back[1:], side, relayed)
    out_relayed = hop(far_sum(out_even, out_got))
    mlp_cores = exchange_cores(mlp_sum.reshape(2, 2, -1, mlp_sum.shape[1]))
    attn_line, last, crossed = stage(attn_line, last, crossed)

    attn_sum, mlp_own = reduce_line(attn_line), exchange_chips(mlp_cores)
    out_last, out_crossed = finish(out_odd, out_side, out_relayed)
    input_grad = norm_back((even_back[1], got, last, crossed), layer_input, grad_hidden)
    attn_sum, mlp_own = stage(attn_sum, mlp_own)
    layer_output = (hidden + total((out_even[0], out_got, out_last[:half], out_crossed))).astype(BF)

    def whole(pieces, start, size):
        piece = pieces[..., start : start + size].reshape(4, -1, size)
        return piece.transpose(1, 0, 2).reshape(-1, 4 * size).astype(F32)

    def gain_of(pairs):
        return sum(jnp.sum(w.astype(F32) * g, axis=1) for w, g in pairs)

    size = 2 * part
    core = lax.axis_index("c")
    attn_sum = jnp.where(core == 0, attn_sum, jnp.roll(attn_sum, size, axis=1)).astype(BF)
    attn_cores = exchange_cores(attn_sum.reshape(2, 2, -1, 2 * size))
    starts = (0, units, together(units))
    gate_own, up_own, down_own = (whole(mlp_own, start, units) for start in starts)
    gate_grad, up_grad = gate_own * gain_mlp, up_own * gain_mlp
    mlp_gain = gain_of([(gate_weight, gate_own), (up_weight, up_own)])
    attn_cores, gate_grad, up_grad, down_own, mlp_gain = stage(
        attn_cores, gate_grad, up_grad, down_own, mlp_gain
    )
    attn_own = exchange_chips(attn_cores)

    def attn_whole(kind, start):
        piece = attn_own[:, kind].reshape(2, low_rows, 2, size)[..., start : start + part]
        return piece.transpose(1, 0, 2, 3).reshape(low_rows, 4 * part).astype(F32)

    query_own, key_own, value_own, output_own = (
        attn_whole(kind, start) for kind in (0, 1) for start in (0, part)
    )
    gains = jnp.stack(
        [
            gain_of([(query_weight, query_own), (key_weight, key_own), (value_weight, value_own)]),
            mlp_gain,
        ]
    )
    attn_gain, mlp_gain = gains + swap(gains, "t")
    return (
        layer_output,
        input_grad,
        attn_gain,
        query_own * gain_attn,
        key_own * gain_attn,
        value_own * gain_attn,
        output_own.T,
        mlp_gain,
        gate_grad,
        up_grad,
        down_own.T,
    )


def solution(mesh):
    devices = mesh.devices.reshape(4, 4, 2, 2, 2)
    fine = Mesh(devices, ("y", "x", "l", "c", "t"))
    rows = P(GROUP + ("t",), None)
    gain, into, out = P(GROUP), P(GROUP, "t"), P("t", GROUP)
    return jax.shard_map(
        shards,
        mesh=fine,
        in_specs=(rows, gain, into, into, into, out, gain, into, into, out, rows),
        out_specs=(rows, rows, gain, into, into, into, out, gain, into, into, out),
        check_vma=False,
    )
```
